32 devices in a mesh: dp: 8 (over z, x), expert: 4 (over y, core).
Axes of the slice: x: 2, y: 2, z: 4, core: 2. Of those that a mesh axis runs over, the one named last changes fastest.
Arguments:
- tokens: bfloat16 [8192, 1024], P(('dp', 'expert')), may hold values from -6 to 6
- expert_ids: int32 [8192, 2], P(('dp', 'expert')), may hold values from 0 to 31, all different within a row; in each aligned block of 256 rows (0 to 255, 256 to 511, ...) at most 24 rows name the same one
- route_weight: float32 [8192, 2], P(('dp', 'expert')), may hold values from 0.2 to 0.8
- cotangent: bfloat16 [8192, 1024], P(('dp', 'expert')), may hold values from -6 to 6
- w_gate: bfloat16 [32, 1024, 512], P('expert'), may hold values from -0.1875 to 0.1875
- w_up: bfloat16 [32, 1024, 512], P('expert'), may hold values from -0.1875 to 0.1875
- w_down: bfloat16 [32, 512, 1024], P('expert'), may hold values from -0.25 to 0.25
Outputs:
- moe_out: bfloat16 [8192, 1024], P(('dp', 'expert'))
- input_grad: bfloat16 [8192, 1024], P(('dp', 'expert'))
- grad_gate: float32 [32, 1024, 512], P('expert', 'dp')
- grad_up: float32 [32, 1024, 512], P('expert', 'dp')
- grad_down: float32 [32, 512, 1024], P('expert', 'dp')
The draws below stay inside these ranges and needn't reach their ends.
Inputs may be any that keep to these rules, and one draw needn't show every extreme that they name: `expert_ids`: the two ids of a token differ. Among the 256 rows of one device no expert is named by more than 24 rows; in some devices' rows an expert is named by exactly 24.
All inputs are finite; a program needn't handle non-finite values.
Results may differ from the reference program's by a relative error of at most 0.0066.
Values may be sent and summed in bfloat16 or wider, within the bound.
No kernel may reach another device: no remote copies, remote signals or barrier semaphores. Data moves between devices by JAX's collectives and lax.ppermute only.
A program may use at most 192 MiB of HBM per device.

```python
import math
import jax
import jax.numpy as jnp
import numpy as np
from jax import lax

D = 1024
FF = 512
EXPERTS = 32
TOK_DEV = 256
CAP = 24
TOKENS = 8192


def block_levels(key, extent, split, smallest, high):
    factor_of = 1.0
    for dim, blocks in split:
        heights = jax.random.uniform(jax.random.fold_in(jax.random.fold_in(key, 6), dim), (blocks,), jnp.float32, smallest / len(split), high / len(split))
        factor_of = factor_of * jnp.repeat(jnp.exp(heights), extent[dim] // blocks).reshape((-1,) + (1,) * (len(extent) - 1 - dim))
    return factor_of


def deal_out(stream_key, own, number, rows, number_of, top, limit, lean):
    sequence = jax.random.permutation(stream_key, number_of)
    crowded, common = load_shares(number_of, rows * top, limit, lean, True), load_shares(number_of, rows * top, limit, lean, False)
    places = jnp.arange(number_of)

    def named(lengths, rotation):
        used = int((lengths > 0).sum())
        fixed = max(1, used // 4)
        passed = fixed + (places - fixed + rotation * (used - fixed)) % max(1, number_of - fixed)
        return jnp.zeros((number_of,), jnp.int32).at[sequence[jnp.where(places < fixed, places, passed)]].set(jnp.asarray(lengths, jnp.int32))

    lengths = jnp.where(number % 4 == 0, named(crowded, number // 4), named(common, number - number // 4 - 1))
    mixed = jax.random.permutation(jax.random.fold_in(own, 3), number_of)
    giver, taker = mixed[0:number_of // 2 * 2:2], mixed[1:number_of // 2 * 2:2]
    slack = jnp.minimum(lengths[giver] - 1, limit - lengths[taker]) // 2
    slack = jnp.where((giver == sequence[0]) | (taker == sequence[0]) | (lengths[taker] == 0), 0, jnp.maximum(slack, 0))
    passed = jax.random.randint(jax.random.fold_in(own, 4), (number_of // 2,), 0, 1 << 20) % (slack + 1)
    lengths = lengths.at[giver].add(-passed).at[taker].add(passed)
    labels = jnp.searchsorted(jnp.cumsum(lengths), jnp.arange(rows * top), side="right").astype(jnp.int32)
    listing = labels.reshape(top, rows).T
    listing = listing[jax.random.permutation(jax.random.fold_in(own, 1), rows)]
    rotation = jax.random.randint(jax.random.fold_in(own, 2), (rows, 1), 0, top)
    return jnp.take_along_axis(listing, (jnp.arange(top)[None, :] + rotation) % top, axis=1)


def load_shares(amount, total, bound, skew, full):
    portions = [(1 << 20) // math.isqrt(rank ** skew) + 1 for rank in range(1, amount + 1)]
    largest = bound if full else min(bound, max(-(-total // amount), total * portions[0] // sum(portions)))
    least = 1 if total - largest >= amount - 1 else 0
    counts, spare = [largest] + [least] * (amount - 1), total - largest - least * (amount - 1)
    while spare > 0:
        movable = [i for i in range(1, amount) if counts[i] < largest] or [i for i in range(1, amount) if counts[i] < bound]
        mass, left = sum([portions[i] for i in movable]), spare
        for i in movable:
            extra = min(bound - counts[i], max(1, left * portions[i] // mass), spare)
            counts[i] = counts[i] + extra
            spare = spare - extra
    return np.array(counts)


def normal_values(stream_key, extent, deviation, reach, split=(), kind=jnp.bfloat16):
    values = jax.random.normal(stream_key, extent, jnp.float32) * deviation
    if len(split) > 0:
        values = block_levels(stream_key, extent, split, -0.22, 0.18) * values
    return jnp.clip(values, min=-reach, max=reach).astype(kind)


def setup_inputs(seed: int = 0) -> dict:
    seeds = jax.random.split(jax.random.key(seed), 8)
    tokens = normal_values(seeds[0], (TOKENS, D), 1.0, 6.0, ((0, 32),))
    expert_ids_keys = jax.random.split(jax.random.fold_in(seeds[1], 1), TOKENS // TOK_DEV)
    expert_ids_turns = jax.random.permutation(jax.random.fold_in(seeds[1], 3), TOKENS // TOK_DEV)
    expert_ids = jax.vmap(lambda own, number: deal_out(jax.random.fold_in(seeds[1], 2), own, number, TOK_DEV, EXPERTS, 2, CAP, 1))(expert_ids_keys, expert_ids_turns).reshape((TOKENS, 2))
    route_weight = jnp.clip(0.2 + 0.6 * jax.random.uniform(seeds[2], (TOKENS, 2), jnp.float32) ** block_levels(seeds[2], (TOKENS, 2), ((0, 32),), -0.2, 0.2), 0.2, 0.8)
    cotangent = normal_values(seeds[3], (TOKENS, D), 1.0, 6.0, ((0, 32),))
    w_gate = normal_values(seeds[4], (EXPERTS, D, FF), D ** -0.5, 0.1875, ((0, 4),))
    w_up = normal_values(seeds[5], (EXPERTS, D, FF), D ** -0.5, 0.1875, ((0, 4),))
    w_down = normal_values(seeds[6], (EXPERTS, FF, D), FF ** -0.5, 0.25, ((0, 4),))
    return dict(tokens=tokens, expert_ids=expert_ids, route_weight=route_weight, cotangent=cotangent, w_gate=w_gate, w_up=w_up, w_down=w_down)


def slots_of(expert_ids):
    blocks = TOKENS // TOK_DEV
    flat = expert_ids.reshape(blocks, 2 * TOK_DEV)
    onehot = (flat[:, :, None] == jnp.arange(EXPERTS, dtype=jnp.int32)[None, None, :]).astype(jnp.int32)
    before = jnp.cumsum(onehot, axis=1) - onehot
    return jnp.sum(before * onehot, axis=2).astype(jnp.int32).reshape(TOKENS, 2)


def per_expert(inputs):
    rows, drows, wg, wu, wd = inputs
    x32 = rows.astype(jnp.float32)
    d32 = drows.astype(jnp.float32)
    wg32 = wg.astype(jnp.float32)
    wu32 = wu.astype(jnp.float32)
    wd32 = wd.astype(jnp.float32)
    gate = jnp.dot(x32, wg32)
    up = jnp.dot(x32, wu32)
    sig = jax.nn.sigmoid(gate)
    hidden = (gate * sig * up).astype(jnp.bfloat16)
    hid32 = hidden.astype(jnp.float32)
    out = jnp.dot(hid32, wd32).astype(jnp.bfloat16)
    dh = jnp.dot(d32, wd32.T)
    dgate = (dh * up * sig * (1.0 + gate * (1.0 - sig))).astype(jnp.bfloat16).astype(jnp.float32)
    dup = (dh * gate * sig).astype(jnp.bfloat16).astype(jnp.float32)
    dx = (jnp.dot(dgate, wg32.T) + jnp.dot(dup, wu32.T)).astype(jnp.bfloat16)
    return out, dx, jnp.dot(x32.T, dgate), jnp.dot(x32.T, dup), jnp.dot(hid32.T, d32)


def reference(tokens, expert_ids, route_weight, cotangent, w_gate, w_up, w_down):
    blocks = TOKENS // TOK_DEV
    slot = slots_of(expert_ids)
    owner = (jnp.arange(TOKENS, dtype=jnp.int32) // TOK_DEV)[:, None]
    pos = (owner * CAP + slot).astype(jnp.int32)
    width = blocks * CAP
    pair = jnp.broadcast_to(tokens[:, None, :], (TOKENS, 2, D))
    rows = jnp.zeros((EXPERTS, width, D), jnp.bfloat16).at[expert_ids, pos].set(pair)
    scaled = (route_weight[:, :, None] * cotangent[:, None, :].astype(jnp.float32)).astype(jnp.bfloat16)
    drows = jnp.zeros((EXPERTS, width, D), jnp.bfloat16).at[expert_ids, pos].set(scaled)
    out, dx, grad_gate, grad_up, grad_down = lax.map(per_expert, (rows, drows, w_gate, w_up, w_down))
    picked = out[expert_ids, pos].astype(jnp.float32)
    moe_out = jnp.sum(route_weight[:, :, None] * picked, axis=1).astype(jnp.bfloat16)
    input_grad = jnp.sum(dx[expert_ids, pos].astype(jnp.float32), axis=1).astype(jnp.bfloat16)
    return moe_out, input_grad, grad_gate, grad_up, grad_down
```

```python
import functools

import jax
import jax.numpy as jnp
from jax import lax
from jax.experimental import pallas as pl
from jax.experimental.pallas import tpu as pltpu
from jax.sharding import PartitionSpec as P

EXPERTS = 32
CAP = 24
VMEM_LIMIT = 56 * 1024 * 1024


def route_kernel(ids_ref, rw_ref, out_ref):
    toks = ids_ref.shape[1]
    ids0, ids1 = ids_ref[0:1, :], ids_ref[1:2, :]
    expert = lax.broadcasted_iota(jnp.int32, (EXPERTS, toks), 0)
    hot0 = (expert == ids0).astype(jnp.float32)
    hot1 = (expert == ids1).astype(jnp.float32)
    row = lax.broadcasted_iota(jnp.int32, (toks, toks), 0)
    col = lax.broadcasted_iota(jnp.int32, (toks, toks), 1)
    earlier = (row < col).astype(jnp.bfloat16)
    before = jnp.dot(
        (hot0 + hot1).astype(jnp.bfloat16), earlier, preferred_element_type=jnp.float32
    )
    slot0 = jnp.sum(before * hot0, axis=0, keepdims=True)
    slot1 = jnp.sum(before * hot1, axis=0, keepdims=True)
    out_ref[0:1, :] = ids0.astype(jnp.float32) * CAP + slot0
    out_ref[1:2, :] = ids1.astype(jnp.float32) * CAP + slot1
    out_ref[2:4, :] = rw_ref[...]


def route(expert_ids, route_weight):
    toks = expert_ids.shape[0]
    return pl.pallas_call(
        route_kernel,
        out_shape=jax.ShapeDtypeStruct((4, toks), jnp.float32),
    )(expert_ids.T, route_weight.T)


def pick_matrix(meta, base, slots):
    toks = meta.shape[1]
    place = lax.broadcasted_iota(jnp.int32, (slots, toks), 0)
    at0 = meta[0:1, :].astype(jnp.int32) - base
    at1 = meta[1:2, :].astype(jnp.int32) - base
    hit0, hit1 = place == at0, place == at1
    hot = jnp.where(hit0 | hit1, 1.0, 0.0).astype(jnp.bfloat16)
    weight = jnp.where(hit0, meta[2:3, :], 0.0) + jnp.where(hit1, meta[3:4, :], 0.0)
    return hot, jnp.sum(weight, axis=1, keepdims=True)


def dot(a, b, dims):
    return lax.dot_general(a, b, (dims, ((), ())), preferred_element_type=jnp.float32)


NN = ((1,), (0,))
NT = ((1,), (1,))
TN = ((0,), (0,))


def rows_kernel(parts, blocks, local_exp, home, first, sp_ref, meta_ref, *refs):
    n_arr = sum(len(p) for p in parts)
    arrays, refs = refs[:n_arr], refs[n_arr:]
    wg_ref, wu_ref, wd_ref = refs[:3]
    refs = refs[3:]
    if not first:
        gg_in, gu_in, gd_in = refs[:3]
        refs = refs[3:]
    gg_ref, gu_ref, gd_ref = refs[:3]
    refs = refs[3:]
    if home:
        keep_ref, send_ref = refs[:2]
        refs = refs[2:]
    tok_s, x_s, d_s, h_s, sem = refs[:5]
    if home:
        hot_s, w_s, o_s = refs[5:]

    step = pl.program_id(0)
    pairs = blocks // 2
    slots = local_exp * CAP
    width = x_s.shape[2]
    replica = sp_ref[blocks]
    base = sp_ref[blocks + 1]

    def copies(b):
        out, at = [], sum(len(p) for p in parts[:b])
        lane = 0
        for k, size in enumerate(parts[b]):
            out.append(
                pltpu.make_async_copy(
                    arrays[at + k], tok_s.at[b, :, pl.ds(lane, size)], sem.at[at + k]
                )
            )
            lane += size
        return out

    @pl.when(step == 0)
    def _():
        for b in range(blocks):
            for c in copies(b):
                c.start()

    for p in range(pairs):

        @pl.when(step == p)
        def _():
            for b in (2 * p, 2 * p + 1):
                for c in copies(b):
                    c.wait()

    @pl.when(step < pairs)
    def _():
        hots, weights = [], []
        for k in range(2):
            b = 2 * step + k
            hot, weight = pick_matrix(meta_ref[sp_ref[b]], base, slots)
            if home:
                hot_s[b] = hot
                w_s[b] = weight
            hots.append(hot)
            weights.append(weight)
        at = pl.ds(pl.multiple_of(step * 2 * CAP, 16), 2 * CAP)
        chunk = 512
        for lane in range(0, 2 * width, chunk):
            got = [
                dot(hots[k], tok_s[2 * step + k, :, lane : lane + chunk], NN) for k in range(2)
            ]
            if lane >= width:
                got = [got[k] * weights[k] for k in range(2)]
            for j in range(local_exp):
                rows = jnp.concatenate(
                    [got[k][j * CAP : (j + 1) * CAP] for k in range(2)], axis=0
                ).astype(jnp.bfloat16)
                if lane < width:
                    x_s[j, at, lane : lane + chunk] = rows
                else:
                    d_s[j, at, lane - width : lane - width + chunk] = rows

    @pl.when((step >= pairs) & (step < pairs + local_exp))
    def _():
        j = step - pairs
        x, d = x_s[j], d_s[j]
        wg, wu, wd = wg_ref[0], wu_ref[0], wd_ref[0]
        gate = dot(x, wg, NN)
        up = dot(x, wu, NN)
        dh = dot(d, wd, NT)
        sig = jax.nn.sigmoid(gate)
        act = gate * sig
        hidden = (act * up).astype(jnp.bfloat16)
        dgate = (dh * up * sig * (1.0 + gate * (1.0 - sig))).astype(jnp.bfloat16)
        dup = (dh * act).astype(jnp.bfloat16)
        rows_g = gg_ref.shape[1]
        rows_d = gd_ref.shape[1]
        xs = x_s[j, :, pl.ds(pl.multiple_of(replica * rows_g, 128), rows_g)]
        gg = dot(xs, dgate, TN)
        gu = dot(xs, dup, TN)
        h_s[...] = hidden
        per = 128 // rows_d
        hs = h_s[:, pl.ds(pl.multiple_of(replica // per * 128, 128), 128)]
        wide = dot(hs, d, TN)
        gd = wide[0:rows_d]
        for q in range(1, per):
            gd = jnp.where(replica % per == q, wide[q * rows_d : (q + 1) * rows_d], gd)
        if first:
            gg_ref[0], gu_ref[0], gd_ref[0] = gg, gu, gd
        else:
            gg_ref[0] = gg_in[0] + gg
            gu_ref[0] = gu_in[0] + gu
            gd_ref[0] = gd_in[0] + gd
        if home:
            out = dot(hidden, wd, NN)
            dx = dot(dgate, wg, NT) + dot(dup, wu, NT)
            at = pl.ds(pl.multiple_of(j * CAP, 8), CAP)
            for b in range(blocks):
                mine = slice(b * CAP, (b + 1) * CAP)
                o_s[b, at, :width] = out[mine] * w_s[b, at, :]
                o_s[b, at, width:] = dx[mine]

    if home:

        @pl.when(step >= pairs + local_exp)
        def _():
            b = step - pairs - local_exp
            sums = dot(hot_s[b], o_s[b].astype(jnp.bfloat16), TN).astype(jnp.bfloat16)

            @pl.when(b < blocks // 2)
            def _():
                keep_ref[0] = sums

            @pl.when(b >= blocks // 2)
            def _():
                send_ref[0] = sums


def expert_rows(sources, base, replica, replicas, meta, parts, weights, sums, home):
    w_gate, w_up, w_down = weights
    local_exp, width, ff = w_gate.shape
    blocks = len(parts)
    toks = parts[0][0].shape[0]
    pairs = blocks // 2
    steps = pairs + local_exp + (blocks if home else 0)
    first = sums is None
    slots = local_exp * CAP
    rows = blocks * CAP
    rows_g, rows_d = width // replicas, ff // replicas

    def expert(s, sp):
        return (jnp.clip(s - pairs, 0, local_exp - 1), 0, 0)

    sp = jnp.concatenate([sources, jnp.stack([replica, base])]).astype(jnp.int32)
    arrays = [a for p in parts for a in p]
    sum_shapes = [(local_exp, rows_g, ff), (local_exp, rows_g, ff), (local_exp, rows_d, width)]
    sum_specs = [pl.BlockSpec((1,) + s[1:], expert) for s in sum_shapes]
    in_specs = [pl.BlockSpec(meta.shape, lambda s, sp: (0, 0, 0))]
    in_specs += [pl.BlockSpec(memory_space=pl.ANY)] * len(arrays)
    in_specs += [
        pl.BlockSpec((1, width, ff), expert),
        pl.BlockSpec((1, width, ff), expert),
        pl.BlockSpec((1, ff, width), expert),
    ]
    operands = [sp, meta, *arrays, w_gate, w_up, w_down]
    aliases = {}
    if not first:
        aliases = {len(operands) + k: k for k in range(3)}
        in_specs += sum_specs
        operands += list(sums)
    out_shape = [jax.ShapeDtypeStruct(s, jnp.float32) for s in sum_shapes]
    out_specs = list(sum_specs)
    scratch = [
        pltpu.VMEM((blocks, toks, 2 * width), jnp.bfloat16),
        pltpu.VMEM((local_exp, rows, width), jnp.bfloat16),
        pltpu.VMEM((local_exp, rows, width), jnp.bfloat16),
        pltpu.VMEM((rows, ff), jnp.bfloat16),
        pltpu.SemaphoreType.DMA((len(arrays),)),
    ]
    if home:
        half = blocks // 2
        done = pairs + local_exp
        out_shape += [jax.ShapeDtypeStruct((half, toks, 2 * width), jnp.bfloat16)] * 2
        out_specs += [
            pl.BlockSpec(
                (1, toks, 2 * width), lambda s, sp: (jnp.clip(s - done, 0, half - 1), 0, 0)
            ),
            pl.BlockSpec(
                (1, toks, 2 * width), lambda s, sp: (jnp.clip(s - done - half, 0, half - 1), 0, 0)
            ),
        ]
        scratch += [
            pltpu.VMEM((blocks, slots, toks), jnp.bfloat16),
            pltpu.VMEM((blocks, slots, 1), jnp.float32),
            pltpu.VMEM((blocks, slots, 2 * width), jnp.float32),
        ]
    flops = 2 * blocks * slots * toks * 2 * width + 2 * rows * local_exp * width * ff * 5
    kernel = functools.partial(
        rows_kernel,
        tuple(tuple(a.shape[1] for a in p) for p in parts),
        blocks,
        local_exp,
        home,
        first,
    )
    return pl.pallas_call(
        kernel,
        grid_spec=pltpu.PrefetchScalarGridSpec(
            num_scalar_prefetch=1,
            grid=(steps,),
            in_specs=in_specs,
            out_specs=out_specs,
            scratch_shapes=scratch,
        ),
        out_shape=out_shape,
        input_output_aliases=aliases,
        compiler_params=pltpu.CompilerParams(vmem_limit_bytes=VMEM_LIMIT),
        cost_estimate=pl.CostEstimate(
            flops=flops,
            bytes_accessed=3 * local_exp * width * ff * 2 + 12 * width * ff * local_exp // 4,
            transcendentals=rows * local_exp * ff,
        ),
    )(*operands)


def gathered(tokens, expert_ids, route_weight, cotangent, w_gate, w_up, w_down):
    width = tokens.shape[1]
    local_exp = w_gate.shape[0]
    replicas, group = lax.axis_size("dp"), lax.axis_size("expert")
    axes = ("dp", "expert")
    me_dp, me_ex = lax.axis_index("dp"), lax.axis_index("expert")
    z = me_dp // 2

    def permute(value, move):
        pairs = []
        for dp in range(replicas):
            for ex in range(group):
                to = move(dp // 2, dp % 2, ex // 2, ex % 2)
                if to is not None:
                    tz, tx, ty, tc = to
                    pairs.append((dp * group + ex, (tz * 2 + tx) * group + ty * 2 + tc))
        return lax.ppermute(value, axes, pairs)

    over_x = lambda v: permute(v, lambda z, x, y, c: (z, 1 - x, y, c))
    over_y = lambda v: permute(v, lambda z, x, y, c: (z, x, 1 - y, c))
    over_c = lambda v: permute(v, lambda z, x, y, c: (z, x, y, 1 - c))
    near = lambda v: permute(v, lambda z, x, y, c: (z ^ 1, x, y, c))
    mid = lambda v: permute(v, lambda z, x, y, c: (3 - z, x, y, c) if z in (1, 2) else None)
    outward = lambda v: permute(v, lambda z, x, y, c: (z ^ 1, x, y, c) if z in (1, 2) else None)

    meta = lax.all_gather(route(expert_ids, route_weight), axes)
    own = jnp.concatenate([tokens, cotangent], axis=1)

    def source(zs, flip_x, flip_y, flip_c):
        dp = zs * 2 + (me_dp % 2) ^ flip_x
        ex = me_ex ^ (flip_y * 2 + flip_c)
        return dp * group + ex

    def plane(block, zs):
        bx, by = over_x(block), over_y(block)
        diag_x = over_y(bx[:, :width])
        diag_d = over_x(by[:, width:])
        blocks = {(0, 0): (block,), (0, 1): (by,), (1, 0): (bx,), (1, 1): (diag_x, diag_d)}
        columns = []
        for fx in range(2):
            parts, sources = [], []
            for fc in range(2):
                for fy in range(2):
                    arrays = blocks[fx, fy]
                    parts.append(tuple(over_c(a) for a in arrays) if fc else arrays)
                    sources.append(source(zs, fx, fy, fc))
            columns.append((parts, sources))
        return columns

    inner = (z == 1) | (z == 2)
    d1 = near(own)
    m1 = mid(own)
    m2 = mid(d1)
    e1 = outward(m1)
    e2 = outward(m2)
    second = jnp.where(inner, m1, e1)
    third = jnp.where(inner, m2, e2)
    z_second = jnp.where(z < 2, 2, 1)
    z_third = jnp.where(z < 2, 3, 0)

    plane0 = plane(own, z)
    plane1 = plane(d1, z ^ 1)
    plane2 = plane(second, z_second)
    plane3 = plane(third, z_third)

    weights = (w_gate, w_up, w_down)

    def rows(columns, sums, home=False):
        parts = [p for c in columns for p in c[0]]
        sources = jnp.stack([s for c in columns for s in c[1]])
        return expert_rows(
            sources, me_ex * local_exp * CAP, me_dp, replicas, meta, parts, weights, sums, home
        )

    *sums, keep, send = rows(plane0[:1], None, home=True)
    got = over_c(send)
    both = keep.astype(jnp.float32) + got.astype(jnp.float32)
    back = over_y(both[1].astype(jnp.bfloat16))
    total = (both[0] + back.astype(jnp.float32)).astype(jnp.bfloat16)
    sums = rows(plane0[1:] + plane1, sums)
    sums = rows(plane2, sums)
    sums = rows(plane3, sums)
    return (total[:, :width], total[:, width:], *sums)


def project_in(received, w_gate, w_up):
    gate = jnp.einsum("sjcd,jdf->sjcf", received, w_gate, preferred_element_type=jnp.float32)
    up = jnp.einsum("sjcd,jdf->sjcf", received, w_up, preferred_element_type=jnp.float32)
    return (gate, up)


def exchanged(tokens, expert_ids, route_weight, cotangent, w_gate, w_up, w_down):
    tok_rows, width = tokens.shape
    group = lax.axis_size("expert")
    local_exp = w_gate.shape[0]
    flat_ids = expert_ids.reshape(-1)
    onehot = (flat_ids[:, None] == jnp.arange(EXPERTS, dtype=jnp.int32)[None, :]).astype(jnp.int32)
    slot = jnp.sum((jnp.cumsum(onehot, axis=0) - onehot) * onehot, axis=1)
    target = flat_ids * CAP + slot
    token_pair = jnp.broadcast_to(tokens[:, None, :], (tok_rows, 2, width)).reshape(
        2 * tok_rows, width
    )
    outgoing = jnp.zeros((EXPERTS * CAP, width), jnp.bfloat16).at[target].set(token_pair)
    outgoing = outgoing.reshape(group, local_exp, CAP, width)
    received = lax.all_to_all(outgoing, "expert", split_axis=0, concat_axis=0, tiled=True)
    gate, up = project_in(received, w_gate, w_up)
    sig = jax.nn.sigmoid(gate)
    hidden = (gate * sig * up).astype(jnp.bfloat16)
    expert_out = jnp.einsum(
        "sjcf,jfd->sjcd", hidden, w_down, preferred_element_type=jnp.float32
    ).astype(jnp.bfloat16)
    returned = lax.all_to_all(
        expert_out, "expert", split_axis=0, concat_axis=0, tiled=True
    ).reshape(EXPERTS * CAP, width)
    picked = returned[target].reshape(tok_rows, 2, width).astype(jnp.float32)
    moe_out = jnp.sum(route_weight[:, :, None] * picked, axis=1).astype(jnp.bfloat16)
    cot_pair = jnp.broadcast_to(cotangent[:, None, :], (tok_rows, 2, width)).reshape(
        2 * tok_rows, width
    )
    scaled = (route_weight.reshape(-1)[:, None] * cot_pair.astype(jnp.float32)).astype(jnp.bfloat16)
    grad_out = jnp.zeros((EXPERTS * CAP, width), jnp.bfloat16).at[target].set(scaled)
    grad_out = grad_out.reshape(group, local_exp, CAP, width)
    drows = lax.all_to_all(grad_out, "expert", split_axis=0, concat_axis=0, tiled=True)
    dh = jnp.einsum("sjcd,jfd->sjcf", drows, w_down, preferred_element_type=jnp.float32)
    dgate = (dh * up * sig * (1.0 + gate * (1.0 - sig))).astype(jnp.bfloat16)
    dup = (dh * gate * sig).astype(jnp.bfloat16)
    dx_rows = jnp.einsum("sjcf,jdf->sjcd", dgate, w_gate, preferred_element_type=jnp.float32)
    dx_rows = (
        dx_rows + jnp.einsum("sjcf,jdf->sjcd", dup, w_up, preferred_element_type=jnp.float32)
    ).astype(jnp.bfloat16)
    dx_back = lax.all_to_all(dx_rows, "expert", split_axis=0, concat_axis=0, tiled=True).reshape(
        EXPERTS * CAP, width
    )
    input_grad = jnp.sum(
        dx_back[target].reshape(tok_rows, 2, width).astype(jnp.float32), axis=1
    ).astype(jnp.bfloat16)
    full_gate = jnp.einsum("sjcd,sjcf->jdf", received, dgate, preferred_element_type=jnp.float32)
    full_up = jnp.einsum("sjcd,sjcf->jdf", received, dup, preferred_element_type=jnp.float32)
    full_down = jnp.einsum("sjcf,sjcd->jfd", hidden, drows, preferred_element_type=jnp.float32)
    grads = [
        lax.psum_scatter(g, "dp", scatter_dimension=1, tiled=True)
        for g in (full_gate, full_up, full_down)
    ]
    return (moe_out, input_grad, *grads)


def solution(mesh):
    placed = (
        P(("dp", "expert"), None),
        P(("dp", "expert"), None),
        P(("dp", "expert"), None),
        P(("dp", "expert"), None),
        P("expert", None, None),
        P("expert", None, None),
        P("expert", None, None),
    )
    small = mesh.shape["dp"] == 8 and mesh.shape["expert"] == 4
    return jax.shard_map(
        gathered if small else exchanged,
        mesh=mesh,
        in_specs=placed,
        out_specs=(
            P(("dp", "expert"), None),
            P(("dp", "expert"), None),
            P("expert", "dp", None),
            P("expert", "dp", None),
            P("expert", "dp", None),
        ),
        check_vma=False,
    )
```

```python
import functools

import jax
import jax.numpy as jnp
from jax import lax
from jax.experimental import pallas as pl
from jax.experimental.pallas import tpu as pltpu
from jax.sharding import PartitionSpec as P

EXPERTS = 32
CAP = 24
VMEM_LIMIT = 28 * 1024 * 1024
SMALL_VMEM = 4 * 1024 * 1024


def route_kernel(ids_ref, rw_ref, out_ref):
    toks = ids_ref.shape[1]
    ids0, ids1 = ids_ref[0:1, :], ids_ref[1:2, :]
    expert = lax.broadcasted_iota(jnp.int32, (EXPERTS, toks), 0)
    hot0 = (expert == ids0).astype(jnp.float32)
    hot1 = (expert == ids1).astype(jnp.float32)
    row = lax.broadcasted_iota(jnp.int32, (toks, toks), 0)
    col = lax.broadcasted_iota(jnp.int32, (toks, toks), 1)
    earlier = (row < col).astype(jnp.bfloat16)
    before = jnp.dot(
        (hot0 + hot1).astype(jnp.bfloat16), earlier, preferred_element_type=jnp.float32
    )
    slot0 = jnp.sum(before * hot0, axis=0, keepdims=True)
    slot1 = jnp.sum(before * hot1, axis=0, keepdims=True)
    out_ref[0:1, :] = ids0.astype(jnp.float32) * CAP + slot0
    out_ref[1:2, :] = ids1.astype(jnp.float32) * CAP + slot1
    out_ref[2:4, :] = rw_ref[...]


def route(expert_ids, route_weight):
    toks = expert_ids.shape[0]
    return pl.pallas_call(
        route_kernel,
        out_shape=jax.ShapeDtypeStruct((4, toks), jnp.float32),
        compiler_params=pltpu.CompilerParams(vmem_limit_bytes=SMALL_VMEM),
    )(expert_ids.T, route_weight.T)


SMALL = pltpu.CompilerParams(vmem_limit_bytes=SMALL_VMEM)
FREE = pl.CostEstimate(flops=1, bytes_accessed=1, transcendentals=0)
VMEM = pl.BlockSpec(memory_space=pltpu.VMEM)
ANY = pl.BlockSpec(memory_space=pl.ANY)


def position():
    return lax.axis_index("dp"), lax.axis_index("expert")


def is_inner():
    z = position()[0] // 2
    return (z == 1) | (z == 2)


def join(a, b):
    def kernel(a_ref, b_ref, out_ref):
        out_ref[: a.shape[0]] = a_ref[...]
        out_ref[a.shape[0] :] = b_ref[...]

    return pl.pallas_call(
        kernel,
        in_specs=[VMEM] * 2,
        out_specs=VMEM,
        out_shape=jax.ShapeDtypeStruct((2 * a.shape[0],) + a.shape[1:], a.dtype),
        compiler_params=SMALL,
    )(a, b)


def pack(by, bx, block, at_ends=None):
    rows, width = block.shape[0], block.shape[1] // 2
    half = rows // 2
    choices = [block] if at_ends is None else [block, at_ends]

    def kernel(by_ref, bx_ref, *refs):
        block_refs, (px_ref, py_ref, sem) = refs[:-3], refs[-3:]
        copies = []
        for out_ref, ref, lane in ((px_ref, by_ref, width), (py_ref, bx_ref, 0)):
            for k in range(2):
                src = ref.at[pl.ds(k * half, half), pl.ds(lane, width)]
                copies.append((src, out_ref.at[pl.ds(rows, half), pl.ds(k * width, width)]))
        copies = [pltpu.make_async_copy(src, dst, sem.at[k]) for k, (src, dst) in enumerate(copies)]

        def tops(block_ref):
            return [
                pltpu.make_async_copy(block_ref, out_ref.at[pl.ds(0, rows)], sem.at[4 + k])
                for k, out_ref in enumerate((px_ref, py_ref))
            ]

        if len(block_refs) == 1:
            for c in tops(block_refs[0]):
                c.start()
        else:
            inner = is_inner()

            @pl.when(inner)
            def _():
                for c in tops(block_refs[0]):
                    c.start()

            @pl.when(jnp.logical_not(inner))
            def _():
                for c in tops(block_refs[1]):
                    c.start()

        for c in copies:
            c.start()
        for c in copies + tops(block_refs[0]):
            c.wait()

    return pl.pallas_call(
        kernel,
        in_specs=[ANY] * (2 + len(choices)),
        out_specs=[ANY] * 2,
        out_shape=[jax.ShapeDtypeStruct((rows + half, 2 * width), block.dtype)] * 2,
        scratch_shapes=[pltpu.SemaphoreType.DMA((6,))],
        compiler_params=SMALL,
    )(*in_hbm([by, bx, *choices]))


def halves(a, b):
    rows, width = a.shape[0] * 2 // 3, a.shape[1] // 2

    def kernel(a_ref, b_ref, left_ref, right_ref, sem):
        top = pl.ds(0, rows)
        left = pltpu.make_async_copy(a_ref.at[top, pl.ds(0, width)], left_ref, sem.at[0])
        right = pltpu.make_async_copy(b_ref.at[top, pl.ds(width, width)], right_ref, sem.at[1])
        left.start()
        right.start()
        left.wait()
        right.wait()

    return pl.pallas_call(
        kernel,
        in_specs=[ANY] * 2,
        out_specs=[ANY] * 2,
        out_shape=[jax.ShapeDtypeStruct((rows, width), a.dtype)] * 2,
        scratch_shapes=[pltpu.SemaphoreType.DMA((2,))],
        compiler_params=SMALL,
    )(*in_hbm([a, b]))


def core_sum(keep, got):
    def kernel(keep_ref, got_ref, mine_ref, away_ref):
        mine_ref[...] = keep_ref[0].astype(jnp.float32) + got_ref[0].astype(jnp.float32)
        away_ref[...] = (keep_ref[1].astype(jnp.float32) + got_ref[1].astype(jnp.float32)).astype(
            away_ref.dtype
        )

    shape = keep.shape[1:]
    return pl.pallas_call(
        kernel,
        in_specs=[VMEM] * 2,
        out_specs=[VMEM] * 2,
        out_shape=[jax.ShapeDtypeStruct(shape, jnp.float32), jax.ShapeDtypeStruct(shape, keep.dtype)],
        compiler_params=pltpu.CompilerParams(vmem_limit_bytes=3 * SMALL_VMEM),
    )(*in_hbm([keep, got]))


def chip_sum(mine, back):
    rows, width = mine.shape[0], mine.shape[1] // 2

    def kernel(mine_ref, back_ref, out_ref, grad_ref):
        total = (mine_ref[...] + back_ref[...].astype(jnp.float32)).astype(out_ref.dtype)
        out_ref[...] = total[:, :width]
        grad_ref[...] = total[:, width:]

    part = rows // 4
    wide = pl.BlockSpec((part, 2 * width), lambda i: (i, 0))
    narrow = pl.BlockSpec((part, width), lambda i: (i, 0))
    return pl.pallas_call(
        kernel,
        grid=(4,),
        in_specs=[wide] * 2,
        out_specs=[narrow] * 2,
        out_shape=[jax.ShapeDtypeStruct((rows, width), back.dtype)] * 2,
        compiler_params=pltpu.CompilerParams(vmem_limit_bytes=3 * SMALL_VMEM),
    )(*in_hbm([mine, back]))


def in_hbm(arrays):
    return [pltpu.with_memory_space_constraint(a, pltpu.HBM) for a in arrays]


def in_vmem(arrays):
    return [pltpu.with_memory_space_constraint(a, pltpu.VMEM) for a in arrays]


def load(*arrays):
    count, parts = len(arrays), arrays[0].shape[0]

    def kernel(*refs):
        sem = refs[-1]
        copies = [
            pltpu.make_async_copy(refs[k].at[j], refs[count + k].at[j], sem.at[k, j])
            for j in range(parts)
            for k in range(count)
        ]
        for c in copies:
            c.start()
        for c in copies:
            c.wait()

    return pl.pallas_call(
        kernel,
        in_specs=[ANY] * count,
        out_specs=[VMEM] * count,
        out_shape=[pltpu.VMEM(a.shape, a.dtype) for a in arrays],
        scratch_shapes=[pltpu.SemaphoreType.DMA((count, parts))],
        compiler_params=SMALL,
        cost_estimate=FREE,
    )(*in_hbm(arrays))


def pick_matrix(meta, base, slots):
    toks = meta.shape[1]
    place = lax.broadcasted_iota(jnp.int32, (slots, toks), 0)
    at0 = meta[0:1, :].astype(jnp.int32) - base
    at1 = meta[1:2, :].astype(jnp.int32) - base
    hit0, hit1 = place == at0, place == at1
    hot = jnp.where(hit0 | hit1, 1.0, 0.0).astype(jnp.bfloat16)
    weight = jnp.where(hit0, meta[2:3, :], 0.0) + jnp.where(hit1, meta[3:4, :], 0.0)
    return hot, jnp.sum(weight, axis=1, keepdims=True)


def dot(a, b, dims):
    return lax.dot_general(a, b, (dims, ((), ())), preferred_element_type=jnp.float32)


NN = ((1,), (0,))
NT = ((1,), (1,))
TN = ((0,), (0,))


def rows_kernel(pieces, n_arr, places, home, first, last, meta_ref, *refs):
    blocks = len(places)
    arrays, refs = refs[:n_arr], refs[n_arr:]
    wg_ref, wu_ref, wd_ref = refs[:3]
    refs = refs[3:]
    if not first:
        gg_in, gu_in, gd_in = refs[:3]
        refs = refs[3:]
    outs = refs[:3]
    refs = refs[3:]
    if home:
        keep_ref, send_ref = refs[:2]
        refs = refs[2:]
    tok_s, x_s, d_s, h_s, sem = refs[:5]
    refs = refs[5:]
    if last:
        sums, sem_out = refs[:3], refs[3]
        refs = refs[4:]
    else:
        sums = outs
    gg_ref, gu_ref, gd_ref = sums
    if home:
        hot_s, w_s, o_s = refs

    local_exp, width, ff = wg_ref.shape
    slots = local_exp * CAP
    replica, group = position()
    inner = is_inner()
    planes = (0, 4, jnp.where(inner, 20, 16), jnp.where(inner, 16, 20))
    sources = [planes[plane] + rest for plane, rest in places]
    base = group * slots

    for b in range(blocks):
        for k, (sr, sc), (dr, dc), (nr, nc) in pieces[b]:
            src = arrays[k].at[pl.ds(sr, nr), pl.ds(sc, nc)]
            dst = tok_s.at[b, pl.ds(dr, nr), pl.ds(dc, nc)]
            pltpu.make_async_copy(src, dst, sem.at[b]).start()

    def gather(p, carry):
        hots, weights = [], []
        for k in range(2):
            b = 2 * p + k
            source = sources[k]
            for q in range(1, blocks // 2):
                source = jnp.where(p == q, sources[2 * q + k], source)
            pltpu.make_async_copy(tok_s.at[b], tok_s.at[b], sem.at[b]).wait()
            hot, weight = pick_matrix(meta_ref[source], base, slots)
            if home:
                hot_s[b] = hot
                w_s[b] = weight
            hots.append(hot)
            weights.append(weight)
        to = pl.ds(pl.multiple_of(p * 2 * CAP, 16), 2 * CAP)
        chunk = 512
        for lane in range(0, 2 * width, chunk):
            got = [dot(hots[k], tok_s[2 * p + k, :, lane : lane + chunk], NN) for k in range(2)]
            if lane >= width:
                got = [got[k] * weights[k] for k in range(2)]
            for j in range(local_exp):
                rows = jnp.concatenate(
                    [got[k][j * CAP : (j + 1) * CAP] for k in range(2)], axis=0
                ).astype(jnp.bfloat16)
                if lane < width:
                    x_s[j, to, lane : lane + chunk] = rows
                else:
                    d_s[j, to, lane - width : lane - width + chunk] = rows
        return carry

    lax.fori_loop(0, blocks // 2, gather, 0)

    def expert(j, carry):
        x, d = x_s[j], d_s[j]
        wg, wu, wd = wg_ref[j], wu_ref[j], wd_ref[j]
        gate = dot(x, wg, NN)
        up = dot(x, wu, NN)
        dh = dot(d, wd, NT)
        sig = jax.nn.sigmoid(gate)
        act = gate * sig
        hidden = (act * up).astype(jnp.bfloat16)
        dgate = (dh * up * sig * (1.0 + gate * (1.0 - sig))).astype(jnp.bfloat16)
        dup = (dh * act).astype(jnp.bfloat16)
        rows_g = gg_ref.shape[1]
        rows_d = gd_ref.shape[1]
        xs = x_s[j, :, pl.ds(pl.multiple_of(replica * rows_g, 128), rows_g)]
        gg = dot(xs, dgate, TN)
        gu = dot(xs, dup, TN)
        h_s[...] = hidden
        per = 128 // rows_d
        hs = h_s[:, pl.ds(pl.multiple_of(replica // per * 128, 128), 128)]
        wide = dot(hs, d, TN)
        gd = wide[0:rows_d]
        for q in range(1, per):
            gd = jnp.where(replica % per == q, wide[q * rows_d : (q + 1) * rows_d], gd)
        if first:
            gg_ref[j], gu_ref[j], gd_ref[j] = gg, gu, gd
        else:
            gg_ref[j] = gg_in[j] + gg
            gu_ref[j] = gu_in[j] + gu
            gd_ref[j] = gd_in[j] + gd
        if last:
            for k in range(3):
                pltpu.make_async_copy(sums[k].at[j], outs[k].at[j], sem_out.at[k, j]).start()
        if home:
            out = dot(hidden, wd, NN)
            dx = dot(dgate, wg, NT) + dot(dup, wu, NT)
            to = pl.ds(pl.multiple_of(j * CAP, 8), CAP)
            for b in range(blocks):
                mine = slice(b * CAP, (b + 1) * CAP)
                o_s[b, to, :width] = out[mine] * w_s[b, to, :]
                o_s[b, to, width:] = dx[mine]
        return carry

    lax.fori_loop(0, local_exp, expert, 0)

    if home:
        half = blocks // 2
        for b in range(blocks):
            got = dot(hot_s[b], o_s[b].astype(jnp.bfloat16), TN).astype(jnp.bfloat16)
            if b < half:
                keep_ref[b] = got
            else:
                send_ref[b - half] = got
    if last:
        for j in range(local_exp):
            for k in range(3):
                pltpu.make_async_copy(sums[k].at[j], outs[k].at[j], sem_out.at[k, j]).wait()


def expert_rows(places, replicas, meta, parts, weights, sums, home=False, last=False):
    local_exp, width, ff = weights[0].shape
    blocks = len(parts)
    toks = meta.shape[2]
    first = sums is None
    slots = local_exp * CAP
    rows = blocks * CAP
    rows_g, rows_d = width // replicas, ff // replicas
    arrays, pieces = [], []
    for part in parts:
        mine = []
        for array, *where in part:
            found = [k for k, a in enumerate(arrays) if a is array]
            if not found:
                arrays.append(array)
            mine.append((found[0] if found else len(arrays) - 1, *where))
        pieces.append(tuple(mine))
    sum_shapes = [(local_exp, rows_g, ff), (local_exp, rows_g, ff), (local_exp, rows_d, width)]
    in_specs = [VMEM] + [ANY] * len(arrays) + [VMEM] * 3
    arrays = in_hbm(arrays)
    operands = [meta, *arrays, *in_vmem(weights)]
    aliases = {}
    if not first:
        if not last:
            aliases = {len(operands) + k: k for k in range(3)}
        in_specs += [VMEM] * 3
        operands += in_vmem(sums)
    if last:
        out_shape = [jax.ShapeDtypeStruct(s, jnp.float32) for s in sum_shapes]
        out_specs = [ANY] * 3
    else:
        out_shape = [pltpu.VMEM(s, jnp.float32) for s in sum_shapes]
        out_specs = [VMEM] * 3
    scratch = [
        pltpu.VMEM((blocks, toks, 2 * width), jnp.bfloat16),
        pltpu.VMEM((local_exp, rows, width), jnp.bfloat16),
        pltpu.VMEM((local_exp, rows, width), jnp.bfloat16),
        pltpu.VMEM((rows, ff), jnp.bfloat16),
        pltpu.SemaphoreType.DMA((blocks,)),
    ]
    if last:
        scratch += [pltpu.VMEM(s, jnp.float32) for s in sum_shapes]
        scratch += [pltpu.SemaphoreType.DMA((3, local_exp))]
    if home:
        out_shape += [jax.ShapeDtypeStruct((blocks // 2, toks, 2 * width), jnp.bfloat16)] * 2
        out_specs += [VMEM] * 2
        scratch += [
            pltpu.VMEM((blocks, slots, toks), jnp.bfloat16),
            pltpu.VMEM((blocks, slots, 1), jnp.float32),
            pltpu.VMEM((blocks, slots, 2 * width), jnp.float32),
        ]
    kernel = functools.partial(
        rows_kernel,
        tuple(pieces),
        len(arrays),
        tuple(places),
        home,
        first,
        last,
    )
    return pl.pallas_call(
        kernel,
        in_specs=in_specs,
        out_specs=out_specs,
        scratch_shapes=scratch,
        out_shape=out_shape,
        input_output_aliases=aliases,
        compiler_params=pltpu.CompilerParams(vmem_limit_bytes=VMEM_LIMIT),
        cost_estimate=FREE,
    )(*operands)


def gathered(tokens, expert_ids, route_weight, cotangent, w_gate, w_up, w_down):
    width = tokens.shape[1]
    local_exp = w_gate.shape[0]
    replicas, group = lax.axis_size("dp"), lax.axis_size("expert")
    axes = ("dp", "expert")
    def permute(value, move):
        pairs = []
        for dp in range(replicas):
            for ex in range(group):
                to = move(dp // 2, dp % 2, ex // 2, ex % 2)
                if to is not None:
                    tz, tx, ty, tc = to
                    pairs.append((dp * group + ex, (tz * 2 + tx) * group + ty * 2 + tc))
        return lax.ppermute(value, axes, pairs)

    over_x = lambda v: permute(v, lambda z, x, y, c: (z, 1 - x, y, c))
    over_y = lambda v: permute(v, lambda z, x, y, c: (z, x, 1 - y, c))
    over_c = lambda v: permute(v, lambda z, x, y, c: (z, x, y, 1 - c))
    near = lambda v: permute(v, lambda z, x, y, c: (z ^ 1, x, y, c))
    opposite = lambda v: permute(v, lambda z, x, y, c: (z ^ 2, x, y, c))
    mid = lambda v: permute(v, lambda z, x, y, c: (z ^ 3, x, y, c) if z in (1, 2) else None)
    outward = lambda v: permute(v, lambda z, x, y, c: (z ^ 1, x, y, c) if z in (1, 2) else None)

    own = jnp.concatenate([tokens, cotangent], axis=1)
    toks = own.shape[0]
    half = toks // 2

    def whole(array):
        return ((array, (0, 0), (0, 0), (toks, 2 * width)),)

    def packed(px, py):
        return tuple(
            (array, (toks, k * width), (k * half, lane), (half, width))
            for array, lane in ((py, 0), (px, width))
            for k in range(2)
        )

    def split(left, right):
        return (left, (0, 0), (0, 0), (toks, width)), (right, (0, 0), (0, width), (toks, width))

    def rows(meta, blocks, sums, **kind):
        parts = [b[0] for b in blocks]
        places = [(z, c + y * 2 + x * 8) for _, z, x, c, y in blocks]
        return expert_rows(places, replicas, meta, parts, weights, sums, **kind)

    after = lax.optimization_barrier

    meta = route(expert_ids, route_weight)[None]
    meta_c = over_c(meta)
    bx0, by0, d1, m1 = over_x(own), over_y(own), near(own), mid(own)
    meta = join(meta, meta_c)
    meta_y = over_y(meta)
    weights = load(w_gate, w_up, w_down)

    by0, bx0, d1, m1, meta_y, weights, own_late = after((by0, bx0, d1, m1, meta_y, weights, own))
    px1, py1 = pack(by0, bx0, d1)
    x1, y1, e1, m2 = over_x(px1), over_y(py1), outward(m1), mid(d1)
    meta_home = join(meta, meta_y)
    meta_here = join(meta_home, near(meta_home))
    meta_x = over_x(meta_here)
    own_c, by0_c = over_c(own_late), over_c(by0)
    *sums, keep, send = rows(
        meta_home,
        [
            (whole(own), 0, 0, 0, 0),
            (whole(by0), 0, 0, 0, 1),
            (whole(own_c), 0, 0, 1, 0),
            (whole(by0_c), 0, 0, 1, 1),
        ],
        None,
        home=True,
    )

    keep, send, x1, y1, e1, m2, meta_x, sums = after((keep, send, x1, y1, e1, m2, meta_x, sums))
    px2, py2 = pack(y1, x1, m1, at_ends=e1)
    px2, py2, x1, y1, bx0, d1 = after((px2, py2, x1, y1, bx0, d1))
    x2, y2, e2 = over_x(px2), over_y(py2), outward(m2)
    meta_half = join(meta_here, meta_x)
    meta_far = opposite(meta_half)
    x1_c, y1_c, bx0_c, d1_c = over_c(x1), over_c(y1), over_c(bx0), over_c(d1)
    sums = rows(
        meta_half,
        [
            (whole(bx0), 0, 1, 0, 0),
            (whole(bx0_c), 0, 1, 1, 0),
            (whole(d1), 1, 0, 0, 0),
            (whole(d1_c), 1, 0, 1, 0),
            (whole(x1), 1, 1, 0, 0),
            (whole(x1_c), 1, 1, 1, 0),
            (whole(y1), 1, 0, 0, 1),
            (whole(y1_c), 1, 0, 1, 1),
            (packed(x1, y1), 0, 1, 0, 1),
            (packed(x1_c, y1_c), 0, 1, 1, 1),
        ],
        sums,
    )

    x2, y2, e2, meta_far, sums = after((x2, y2, e2, meta_far, sums))
    px3, py3 = pack(y2, x2, m2, at_ends=e2)
    px3, py3, x2, y2, px2, send = after((px3, py3, x2, y2, px2, send))
    x3, y3 = over_x(px3), over_y(py3)
    meta_all = join(meta_half, meta_far)
    x2_c, y2_c, px2_c, got = over_c(x2), over_c(y2), over_c(px2), over_c(send)
    sums = rows(
        meta_all,
        [
            (whole(px2), 2, 0, 0, 0),
            (whole(px2_c), 2, 0, 1, 0),
            (whole(x2), 2, 1, 0, 0),
            (whole(x2_c), 2, 1, 1, 0),
            (whole(y2), 2, 0, 0, 1),
            (whole(y2_c), 2, 0, 1, 1),
            (packed(x2, y2), 1, 1, 0, 1),
            (packed(x2_c, y2_c), 1, 1, 1, 1),
        ],
        sums,
    )

    x3, y3, got, sums = after((x3, y3, got, sums))
    left, right = halves(x3, y3)
    by_y, by_x = over_y(left), over_x(right)
    mine, away = core_sum(keep, got)
    back = over_y(away)
    x3_c, y3_c, px3_c = over_c(x3), over_c(y3), over_c(px3)
    sums = rows(
        meta_all,
        [
            (whole(px3), 3, 0, 0, 0),
            (whole(px3_c), 3, 0, 1, 0),
            (whole(x3), 3, 1, 0, 0),
            (whole(x3_c), 3, 1, 1, 0),
            (whole(y3), 3, 0, 0, 1),
            (whole(y3_c), 3, 0, 1, 1),
            (packed(x3, y3), 2, 1, 0, 1),
            (packed(x3_c, y3_c), 2, 1, 1, 1),
            (split(by_y, by_x), 3, 1, 0, 1),
            (split(over_c(by_y), over_c(by_x)), 3, 1, 1, 1),
        ],
        sums,
        last=True,
    )
    mine, sums = after((mine, sums))
    moe_out, input_grad = chip_sum(mine, back)
    return (moe_out, input_grad, *sums)


def project_in(received, w_gate, w_up):
    gate = jnp.einsum("sjcd,jdf->sjcf", received, w_gate, preferred_element_type=jnp.float32)
    up = jnp.einsum("sjcd,jdf->sjcf", received, w_up, preferred_element_type=jnp.float32)
    return (gate, up)


def exchanged(tokens, expert_ids, route_weight, cotangent, w_gate, w_up, w_down):
    tok_rows, width = tokens.shape
    group = lax.axis_size("expert")
    local_exp = w_gate.shape[0]
    flat_ids = expert_ids.reshape(-1)
    onehot = (flat_ids[:, None] == jnp.arange(EXPERTS, dtype=jnp.int32)[None, :]).astype(jnp.int32)
    slot = jnp.sum((jnp.cumsum(onehot, axis=0) - onehot) * onehot, axis=1)
    target = flat_ids * CAP + slot
    token_pair = jnp.broadcast_to(tokens[:, None, :], (tok_rows, 2, width)).reshape(
        2 * tok_rows, width
    )
    outgoing = jnp.zeros((EXPERTS * CAP, width), jnp.bfloat16).at[target].set(token_pair)
    outgoing = outgoing.reshape(group, local_exp, CAP, width)
    received = lax.all_to_all(outgoing, "expert", split_axis=0, concat_axis=0, tiled=True)
    gate, up = project_in(received, w_gate, w_up)
    sig = jax.nn.sigmoid(gate)
    hidden = (gate * sig * up).astype(jnp.bfloat16)
    expert_out = jnp.einsum(
        "sjcf,jfd->sjcd", hidden, w_down, preferred_element_type=jnp.float32
    ).astype(jnp.bfloat16)
    returned = lax.all_to_all(
        expert_out, "expert", split_axis=0, concat_axis=0, tiled=True
    ).reshape(EXPERTS * CAP, width)
    picked = returned[target].reshape(tok_rows, 2, width).astype(jnp.float32)
    moe_out = jnp.sum(route_weight[:, :, None] * picked, axis=1).astype(jnp.bfloat16)
    cot_pair = jnp.broadcast_to(cotangent[:, None, :], (tok_rows, 2, width)).reshape(
        2 * tok_rows, width
    )
    scaled = (route_weight.reshape(-1)[:, None] * cot_pair.astype(jnp.float32)).astype(jnp.bfloat16)
    grad_out = jnp.zeros((EXPERTS * CAP, width), jnp.bfloat16).at[target].set(scaled)
    grad_out = grad_out.reshape(group, local_exp, CAP, width)
    drows = lax.all_to_all(grad_out, "expert", split_axis=0, concat_axis=0, tiled=True)
    dh = jnp.einsum("sjcd,jfd->sjcf", drows, w_down, preferred_element_type=jnp.float32)
    dgate = (dh * up * sig * (1.0 + gate * (1.0 - sig))).astype(jnp.bfloat16)
    dup = (dh * gate * sig).astype(jnp.bfloat16)
    dx_rows = jnp.einsum("sjcf,jdf->sjcd", dgate, w_gate, preferred_element_type=jnp.float32)
    dx_rows = (
        dx_rows + jnp.einsum("sjcf,jdf->sjcd", dup, w_up, preferred_element_type=jnp.float32)
    ).astype(jnp.bfloat16)
    dx_back = lax.all_to_all(dx_rows, "expert", split_axis=0, concat_axis=0, tiled=True).reshape(
        EXPERTS * CAP, width
    )
    input_grad = jnp.sum(
        dx_back[target].reshape(tok_rows, 2, width).astype(jnp.float32), axis=1
    ).astype(jnp.bfloat16)
    full_gate = jnp.einsum("sjcd,sjcf->jdf", received, dgate, preferred_element_type=jnp.float32)
    full_up = jnp.einsum("sjcd,sjcf->jdf", received, dup, preferred_element_type=jnp.float32)
    full_down = jnp.einsum("sjcf,sjcd->jfd", hidden, drows, preferred_element_type=jnp.float32)
    grads = [
        lax.psum_scatter(g, "dp", scatter_dimension=1, tiled=True)
        for g in (full_gate, full_up, full_down)
    ]
    return (moe_out, input_grad, *grads)


def solution(mesh):
    placed = (
        P(("dp", "expert"), None),
        P(("dp", "expert"), None),
        P(("dp", "expert"), None),
        P(("dp", "expert"), None),
        P("expert", None, None),
        P("expert", None, None),
        P("expert", None, None),
    )
    small = mesh.shape["dp"] == 8 and mesh.shape["expert"] == 4
    return jax.shard_map(
        gathered if small else exchanged,
        mesh=mesh,
        in_specs=placed,
        out_specs=(
            P(("dp", "expert"), None),
            P(("dp", "expert"), None),
            P("expert", "dp", None),
            P("expert", "dp", None),
            P("expert", "dp", None),
        ),
        check_vma=False,
    )
```

```python
import functools

import jax
import jax.numpy as jnp
from jax import lax
from jax.experimental import pallas as pl
from jax.experimental.pallas import tpu as pltpu
from jax.sharding import PartitionSpec as P

EXPERTS = 32
CAP = 24
VMEM_LIMIT = 24 * 1024 * 1024
SMALL_VMEM = 4 * 1024 * 1024
RING = 6


def route_kernel(ids_ref, rw_ref, out_ref):
    toks = ids_ref.shape[1]
    ids0, ids1 = ids_ref[0:1, :], ids_ref[1:2, :]
    expert = lax.broadcasted_iota(jnp.int32, (EXPERTS, toks), 0)
    hot0 = (expert == ids0).astype(jnp.float32)
    hot1 = (expert == ids1).astype(jnp.float32)
    row = lax.broadcasted_iota(jnp.int32, (toks, toks), 0)
    col = lax.broadcasted_iota(jnp.int32, (toks, toks), 1)
    earlier = (row < col).astype(jnp.bfloat16)
    before = jnp.dot(
        (hot0 + hot1).astype(jnp.bfloat16), earlier, preferred_element_type=jnp.float32
    )
    slot0 = jnp.sum(before * hot0, axis=0, keepdims=True)
    slot1 = jnp.sum(before * hot1, axis=0, keepdims=True)
    out_ref[0:1, :] = ids0.astype(jnp.float32) * CAP + slot0
    out_ref[1:2, :] = ids1.astype(jnp.float32) * CAP + slot1
    out_ref[2:4, :] = rw_ref[...]


def route(expert_ids, route_weight):
    toks = expert_ids.shape[0]
    return pl.pallas_call(
        route_kernel,
        out_shape=jax.ShapeDtypeStruct((4, toks), jnp.float32),
        compiler_params=pltpu.CompilerParams(vmem_limit_bytes=SMALL_VMEM),
    )(expert_ids.T, route_weight.T)


SMALL = pltpu.CompilerParams(vmem_limit_bytes=SMALL_VMEM)
FREE = pl.CostEstimate(flops=1, bytes_accessed=1, transcendentals=0)
VMEM = pl.BlockSpec(memory_space=pltpu.VMEM)
ANY = pl.BlockSpec(memory_space=pl.ANY)


def position():
    return lax.axis_index("dp"), lax.axis_index("expert")


def is_inner():
    z = position()[0] // 2
    return (z == 1) | (z == 2)


def join(a, b):
    def kernel(a_ref, b_ref, out_ref):
        out_ref[: a.shape[0]] = a_ref[...]
        out_ref[a.shape[0] :] = b_ref[...]

    return pl.pallas_call(
        kernel,
        in_specs=[VMEM] * 2,
        out_specs=VMEM,
        out_shape=jax.ShapeDtypeStruct((2 * a.shape[0],) + a.shape[1:], a.dtype),
        compiler_params=SMALL,
    )(a, b)


def pack(by, bx, block, at_ends=None):
    rows, width = block.shape[0], block.shape[1] // 2
    half = rows // 2
    choices = [block] if at_ends is None else [block, at_ends]

    def kernel(by_ref, bx_ref, *refs):
        block_refs, (px_ref, py_ref, sem) = refs[:-3], refs[-3:]
        copies = []
        for out_ref, ref, lane in ((px_ref, by_ref, width), (py_ref, bx_ref, 0)):
            for k in range(2):
                src = ref.at[pl.ds(k * half, half), pl.ds(lane, width)]
                copies.append((src, out_ref.at[pl.ds(rows, half), pl.ds(k * width, width)]))
        copies = [pltpu.make_async_copy(src, dst, sem.at[k]) for k, (src, dst) in enumerate(copies)]

        def tops(block_ref):
            return [
                pltpu.make_async_copy(block_ref, out_ref.at[pl.ds(0, rows)], sem.at[4 + k])
                for k, out_ref in enumerate((px_ref, py_ref))
            ]

        if len(block_refs) == 1:
            for c in tops(block_refs[0]):
                c.start()
        else:
            inner = is_inner()

            @pl.when(inner)
            def _():
                for c in tops(block_refs[0]):
                    c.start()

            @pl.when(jnp.logical_not(inner))
            def _():
                for c in tops(block_refs[1]):
                    c.start()

        for c in copies:
            c.start()
        for c in copies + tops(block_refs[0]):
            c.wait()

    return pl.pallas_call(
        kernel,
        in_specs=[ANY] * (2 + len(choices)),
        out_specs=[VMEM] * 2,
        out_shape=[pltpu.VMEM((rows + half, 2 * width), block.dtype)] * 2,
        scratch_shapes=[pltpu.SemaphoreType.DMA((6,))],
        compiler_params=SMALL,
    )(by, bx, *choices)


def beside(left, right):
    rows, width = left.shape

    def kernel(left_ref, right_ref, out_ref, sem):
        copies = [
            pltpu.make_async_copy(ref, out_ref.at[:, pl.ds(k * width, width)], sem.at[k])
            for k, ref in enumerate((left_ref, right_ref))
        ]
        for c in copies:
            c.start()
        for c in copies:
            c.wait()

    return pl.pallas_call(
        kernel,
        in_specs=[ANY] * 2,
        out_specs=VMEM,
        out_shape=pltpu.VMEM((rows, 2 * width), left.dtype),
        scratch_shapes=[pltpu.SemaphoreType.DMA((2,))],
        compiler_params=SMALL,
        cost_estimate=FREE,
    )(left, right)


def halves(a, b):
    rows, width = a.shape[0] * 2 // 3, a.shape[1] // 2

    def kernel(a_ref, b_ref, left_ref, right_ref, sem):
        top = pl.ds(0, rows)
        left = pltpu.make_async_copy(a_ref.at[top, pl.ds(0, width)], left_ref, sem.at[0])
        right = pltpu.make_async_copy(b_ref.at[top, pl.ds(width, width)], right_ref, sem.at[1])
        left.start()
        right.start()
        left.wait()
        right.wait()

    return pl.pallas_call(
        kernel,
        in_specs=[ANY] * 2,
        out_specs=[VMEM] * 2,
        out_shape=[pltpu.VMEM((rows, width), a.dtype)] * 2,
        scratch_shapes=[pltpu.SemaphoreType.DMA((2,))],
        compiler_params=SMALL,
    )(a, b)


def core_sum(keep, got):
    def kernel(keep_ref, got_ref, mine_ref, away_ref):
        mine_ref[...] = keep_ref[0].astype(jnp.float32) + got_ref[0].astype(jnp.float32)
        away_ref[...] = (keep_ref[1].astype(jnp.float32) + got_ref[1].astype(jnp.float32)).astype(
            away_ref.dtype
        )

    shape = keep.shape[1:]
    return pl.pallas_call(
        kernel,
        in_specs=[VMEM] * 2,
        out_specs=[VMEM] * 2,
        out_shape=[jax.ShapeDtypeStruct(shape, jnp.float32), jax.ShapeDtypeStruct(shape, keep.dtype)],
        compiler_params=pltpu.CompilerParams(vmem_limit_bytes=3 * SMALL_VMEM),
    )(keep, got)


def in_hbm(arrays):
    return [pltpu.with_memory_space_constraint(a, pltpu.HBM) for a in arrays]


def in_vmem(arrays):
    return [pltpu.with_memory_space_constraint(a, pltpu.VMEM) for a in arrays]


def load(*arrays):
    count, parts = len(arrays), arrays[0].shape[0]

    def kernel(*refs):
        sem = refs[-1]
        copies = [
            pltpu.make_async_copy(refs[k].at[j], refs[count + k].at[j], sem.at[k, j])
            for j in range(parts)
            for k in range(count)
        ]
        for c in copies:
            c.start()
        for c in copies:
            c.wait()

    return pl.pallas_call(
        kernel,
        in_specs=[ANY] * count,
        out_specs=[VMEM] * count,
        out_shape=[pltpu.VMEM(a.shape, a.dtype) for a in arrays],
        scratch_shapes=[pltpu.SemaphoreType.DMA((count, parts))],
        compiler_params=SMALL,
        cost_estimate=FREE,
    )(*in_hbm(arrays))


def pick_matrix(meta, base, slots):
    toks = meta.shape[1]
    place = lax.broadcasted_iota(jnp.int32, (slots, toks), 0)
    at0 = meta[0:1, :].astype(jnp.int32) - base
    at1 = meta[1:2, :].astype(jnp.int32) - base
    hit0, hit1 = place == at0, place == at1
    hot = jnp.where(hit0 | hit1, 1.0, 0.0).astype(jnp.bfloat16)
    weight = jnp.where(hit0, meta[2:3, :], 0.0) + jnp.where(hit1, meta[3:4, :], 0.0)
    return hot, jnp.sum(weight, axis=1, keepdims=True)


def dot(a, b, dims):
    return lax.dot_general(a, b, (dims, ((), ())), preferred_element_type=jnp.float32)


NN = ((1,), (0,))
NT = ((1,), (1,))
TN = ((0,), (0,))


def rows_kernel(pieces, n_arr, places, home, first, last, meta_ref, *refs):
    blocks = len(places)
    arrays, refs = refs[:n_arr], refs[n_arr:]
    wg_ref, wu_ref, wd_ref = refs[:3]
    refs = refs[3:]
    if not first:
        gg_in, gu_in, gd_in = refs[:3]
        refs = refs[3:]
    outs = refs[:3]
    refs = refs[3:]
    if home:
        keep_ref, send_ref = refs[:2]
        refs = refs[2:]
    tok_s, x_s, d_s, h_s, sem = refs[:5]
    refs = refs[5:]
    if last:
        sums, sem_out = refs[:3], refs[3]
        refs = refs[4:]
    else:
        sums = outs
    gg_ref, gu_ref, gd_ref = sums
    if home:
        hot_s, w_s, o_s = refs

    local_exp, width, ff = wg_ref.shape
    slots = local_exp * CAP
    replica, group = position()
    inner = is_inner()
    planes = (0, 4, jnp.where(inner, 20, 16), jnp.where(inner, 16, 20))
    sources = [planes[plane] + rest for plane, rest in places]
    base = group * slots

    ring = tok_s.shape[0]

    def fetch(b):
        for k, (sr, sc), (dr, dc), (nr, nc) in pieces[b]:
            src = arrays[k].at[pl.ds(sr, nr), pl.ds(sc, nc)]
            dst = tok_s.at[b % ring, pl.ds(dr, nr), pl.ds(dc, nc)]
            pltpu.make_async_copy(src, dst, sem.at[b % ring]).start()

    for b in range(min(ring, blocks)):
        fetch(b)

    for p in range(blocks // 2):
        pair = (2 * p, 2 * p + 1)
        hots, weights = [], []
        for b in pair:
            hot, weight = pick_matrix(meta_ref[sources[b]], base, slots)
            if home:
                hot_s[b] = hot
                w_s[b] = weight
            hots.append(hot)
            weights.append(weight)
        for b in pair:
            slot = tok_s.at[b % ring]
            pltpu.make_async_copy(slot, slot, sem.at[b % ring]).wait()
        chunk = 512
        for lane in range(0, 2 * width, chunk):
            got = [dot(hots[k], tok_s[pair[k] % ring, :, lane : lane + chunk], NN) for k in range(2)]
            if lane >= width:
                got = [got[k] * weights[k] for k in range(2)]
            for j in range(local_exp):
                rows = jnp.concatenate(
                    [got[k][j * CAP : (j + 1) * CAP] for k in range(2)], axis=0
                ).astype(jnp.bfloat16)
                to = slice(2 * p * CAP, 2 * (p + 1) * CAP)
                if lane < width:
                    x_s[j, to, lane : lane + chunk] = rows
                else:
                    d_s[j, to, lane - width : lane - width + chunk] = rows
        for b in pair:
            if b + ring < blocks:
                fetch(b + ring)

    def expert(j, carry):
        x, d = x_s[j], d_s[j]
        wg, wu, wd = wg_ref[j], wu_ref[j], wd_ref[j]
        gate = dot(x, wg, NN)
        up = dot(x, wu, NN)
        dh = dot(d, wd, NT)
        sig = jax.nn.sigmoid(gate)
        act = gate * sig
        hidden = (act * up).astype(jnp.bfloat16)
        dgate = (dh * up * sig * (1.0 + gate * (1.0 - sig))).astype(jnp.bfloat16)
        dup = (dh * act).astype(jnp.bfloat16)
        rows_g = gg_ref.shape[1]
        rows_d = gd_ref.shape[1]
        xs = x_s[j, :, pl.ds(pl.multiple_of(replica * rows_g, 128), rows_g)]
        gg = dot(xs, dgate, TN)
        gu = dot(xs, dup, TN)
        h_s[...] = hidden
        per = 128 // rows_d
        hs = h_s[:, pl.ds(pl.multiple_of(replica // per * 128, 128), 128)]
        wide = dot(hs, d, TN)
        gd = wide[0:rows_d]
        for q in range(1, per):
            gd = jnp.where(replica % per == q, wide[q * rows_d : (q + 1) * rows_d], gd)
        if first:
            gg_ref[j], gu_ref[j], gd_ref[j] = gg, gu, gd
        else:
            gg_ref[j] = gg_in[j] + gg
            gu_ref[j] = gu_in[j] + gu
            gd_ref[j] = gd_in[j] + gd
        if last:
            for k in range(3):
                pltpu.make_async_copy(sums[k].at[j], outs[k].at[j], sem_out.at[k, j]).start()
        if home:
            out = dot(hidden, wd, NN)
            dx = dot(dgate, wg, NT) + dot(dup, wu, NT)
            to = pl.ds(pl.multiple_of(j * CAP, 8), CAP)
            for b in range(blocks):
                mine = slice(b * CAP, (b + 1) * CAP)
                o_s[b, to, :width] = out[mine] * w_s[b, to, :]
                o_s[b, to, width:] = dx[mine]
        return carry

    lax.fori_loop(0, local_exp, expert, 0)

    if home:
        half = blocks // 2
        for b in range(blocks):
            got = dot(hot_s[b], o_s[b].astype(jnp.bfloat16), TN).astype(jnp.bfloat16)
            if b < half:
                keep_ref[b] = got
            else:
                send_ref[b - half] = got
    if last:
        for j in range(local_exp):
            for k in range(3):
                pltpu.make_async_copy(sums[k].at[j], outs[k].at[j], sem_out.at[k, j]).wait()


def expert_rows(places, replicas, meta, parts, weights, sums, home=False, last=False):
    local_exp, width, ff = weights[0].shape
    blocks = len(parts)
    toks = meta.shape[2]
    first = sums is None
    slots = local_exp * CAP
    rows = blocks * CAP
    rows_g, rows_d = width // replicas, ff // replicas
    arrays, pieces = [], []
    for part in parts:
        mine = []
        for array, *where in part:
            found = [k for k, a in enumerate(arrays) if a is array]
            if not found:
                arrays.append(array)
            mine.append((found[0] if found else len(arrays) - 1, *where))
        pieces.append(tuple(mine))
    sum_shapes = [(local_exp, rows_g, ff), (local_exp, rows_g, ff), (local_exp, rows_d, width)]
    in_specs = [VMEM] + [ANY] * len(arrays) + [VMEM] * 3
    arrays = in_hbm(arrays)
    operands = [meta, *arrays, *in_vmem(weights)]
    aliases = {}
    if not first:
        if not last:
            aliases = {len(operands) + k: k for k in range(3)}
        in_specs += [VMEM] * 3
        operands += in_vmem(sums)
    if last:
        out_shape = [jax.ShapeDtypeStruct(s, jnp.float32) for s in sum_shapes]
        out_specs = [ANY] * 3
    else:
        out_shape = [pltpu.VMEM(s, jnp.float32) for s in sum_shapes]
        out_specs = [VMEM] * 3
    scratch = [
        pltpu.VMEM((min(blocks, RING), toks, 2 * width), jnp.bfloat16),
        pltpu.VMEM((local_exp, rows, width), jnp.bfloat16),
        pltpu.VMEM((local_exp, rows, width), jnp.bfloat16),
        pltpu.VMEM((rows, ff), jnp.bfloat16),
        pltpu.SemaphoreType.DMA((min(blocks, RING),)),
    ]
    if last:
        scratch += [pltpu.VMEM(s, jnp.float32) for s in sum_shapes]
        scratch += [pltpu.SemaphoreType.DMA((3, local_exp))]
    if home:
        out_shape += [jax.ShapeDtypeStruct((blocks // 2, toks, 2 * width), jnp.bfloat16)] * 2
        out_specs += [VMEM] * 2
        scratch += [
            pltpu.VMEM((blocks, slots, toks), jnp.bfloat16),
            pltpu.VMEM((blocks, slots, 1), jnp.float32),
            pltpu.VMEM((blocks, slots, 2 * width), jnp.float32),
        ]
    kernel = functools.partial(
        rows_kernel,
        tuple(pieces),
        len(arrays),
        tuple(places),
        home,
        first,
        last,
    )
    return pl.pallas_call(
        kernel,
        in_specs=in_specs,
        out_specs=out_specs,
        scratch_shapes=scratch,
        out_shape=out_shape,
        input_output_aliases=aliases,
        compiler_params=pltpu.CompilerParams(vmem_limit_bytes=VMEM_LIMIT),
        cost_estimate=FREE,
    )(*operands)


def gathered(tokens, expert_ids, route_weight, cotangent, w_gate, w_up, w_down):
    width = tokens.shape[1]
    local_exp = w_gate.shape[0]
    replicas, group = lax.axis_size("dp"), lax.axis_size("expert")
    axes = ("dp", "expert")
    def permute(value, move):
        pairs = []
        for dp in range(replicas):
            for ex in range(group):
                to = move(dp // 2, dp % 2, ex // 2, ex % 2)
                if to is not None:
                    tz, tx, ty, tc = to
                    pairs.append((dp * group + ex, (tz * 2 + tx) * group + ty * 2 + tc))
        return lax.ppermute(value, axes, pairs)

    over_x = lambda v: permute(v, lambda z, x, y, c: (z, 1 - x, y, c))
    over_y = lambda v: permute(v, lambda z, x, y, c: (z, x, 1 - y, c))
    over_c = lambda v: permute(v, lambda z, x, y, c: (z, x, y, 1 - c))
    near = lambda v: permute(v, lambda z, x, y, c: (z ^ 1, x, y, c))
    opposite = lambda v: permute(v, lambda z, x, y, c: (z ^ 2, x, y, c))
    mid = lambda v: permute(v, lambda z, x, y, c: (z ^ 3, x, y, c) if z in (1, 2) else None)
    outward = lambda v: permute(v, lambda z, x, y, c: (z ^ 1, x, y, c) if z in (1, 2) else None)

    own = beside(tokens, cotangent)
    toks = own.shape[0]
    half = toks // 2

    def whole(array):
        return ((array, (0, 0), (0, 0), (toks, 2 * width)),)

    def packed(px, py):
        return tuple(
            (array, (toks, k * width), (k * half, lane), (half, width))
            for array, lane in ((py, 0), (px, width))
            for k in range(2)
        )

    def split(left, right):
        return (left, (0, 0), (0, 0), (toks, width)), (right, (0, 0), (0, width), (toks, width))

    def rows(meta, blocks, sums, **kind):
        parts = [b[0] for b in blocks]
        places = [(z, c + y * 2 + x * 8) for _, z, x, c, y in blocks]
        return expert_rows(places, replicas, meta, parts, weights, sums, **kind)

    after = lax.optimization_barrier

    meta = route(expert_ids, route_weight)[None]
    meta_c = over_c(meta)
    bx0, by0, d1, m1 = over_x(own), over_y(own), near(own), mid(own)
    meta = join(meta, meta_c)
    meta_y = over_y(meta)
    weights = load(w_gate, w_up, w_down)

    by0, bx0, d1, m1, meta_y, weights, own_late = after((by0, bx0, d1, m1, meta_y, weights, own))
    px1, py1 = pack(by0, bx0, d1)
    x1, y1, e1, m2 = over_x(px1), over_y(py1), outward(m1), mid(d1)
    meta_home = join(meta, meta_y)
    meta_here = join(meta_home, near(meta_home))
    meta_x = over_x(meta_here)
    own_c, by0_c = over_c(own_late), over_c(by0)
    *sums, keep, send = rows(
        meta_home,
        [
            (split(tokens, cotangent), 0, 0, 0, 0),
            (whole(by0), 0, 0, 0, 1),
            (whole(own_c), 0, 0, 1, 0),
            (whole(by0_c), 0, 0, 1, 1),
        ],
        None,
        home=True,
    )

    keep, send, x1, y1, e1, m2, meta_x, sums = after((keep, send, x1, y1, e1, m2, meta_x, sums))
    px2, py2 = pack(y1, x1, m1, at_ends=e1)
    px2, py2, x1, y1, bx0, d1 = after((px2, py2, x1, y1, bx0, d1))
    x2, y2, e2 = over_x(px2), over_y(py2), outward(m2)
    meta_half = join(meta_here, meta_x)
    meta_far = opposite(meta_half)
    x1_c, y1_c, bx0_c, d1_c = over_c(x1), over_c(y1), over_c(bx0), over_c(d1)
    sums = rows(
        meta_half,
        [
            (whole(bx0), 0, 1, 0, 0),
            (whole(bx0_c), 0, 1, 1, 0),
            (whole(x1), 1, 1, 0, 0),
            (whole(x1_c), 1, 1, 1, 0),
            (whole(y1), 1, 0, 0, 1),
            (whole(y1_c), 1, 0, 1, 1),
            (packed(x1, y1), 0, 1, 0, 1),
            (packed(x1_c, y1_c), 0, 1, 1, 1),
        ],
        sums,
    )

    x2, y2, e2, meta_far, d1_c, sums = after((x2, y2, e2, meta_far, d1_c, sums))
    px3, py3 = pack(y2, x2, m2, at_ends=e2)
    px3, py3, x2, y2, px2, send = after((px3, py3, x2, y2, px2, send))
    x3, y3 = over_x(px3), over_y(py3)
    meta_all = join(meta_half, meta_far)
    x2_c, y2_c, px2_c, got = over_c(x2), over_c(y2), over_c(px2), over_c(send)
    mine, away = core_sum(keep, got)
    sums = rows(
        meta_all,
        [
            (whole(d1), 1, 0, 0, 0),
            (whole(d1_c), 1, 0, 1, 0),
            (whole(x2), 2, 1, 0, 0),
            (whole(x2_c), 2, 1, 1, 0),
            (whole(y2), 2, 0, 0, 1),
            (whole(y2_c), 2, 0, 1, 1),
            (packed(x2, y2), 1, 1, 0, 1),
            (packed(x2_c, y2_c), 1, 1, 1, 1),
        ],
        sums,
    )

    x3, y3, away, sums = after((x3, y3, away, sums))
    left, right = halves(x3, y3)
    by_y, by_x = over_y(left), over_x(right)
    back = over_y(away)
    x3_c, y3_c, px3_c = over_c(x3), over_c(y3), over_c(px3)
    sums = rows(
        meta_all,
        [
            (whole(px2), 2, 0, 0, 0),
            (whole(px2_c), 2, 0, 1, 0),
            (whole(px3), 3, 0, 0, 0),
            (whole(px3_c), 3, 0, 1, 0),
            (whole(x3), 3, 1, 0, 0),
            (whole(x3_c), 3, 1, 1, 0),
            (whole(y3), 3, 0, 0, 1),
            (whole(y3_c), 3, 0, 1, 1),
            (packed(x3, y3), 2, 1, 0, 1),
            (packed(x3_c, y3_c), 2, 1, 1, 1),
        ],
        sums,
    )

    by_y, by_x, sums = after((by_y, by_x, sums))
    sums = rows(
        meta_all,
        [
            (split(by_y, by_x), 3, 1, 0, 1),
            (split(over_c(by_y), over_c(by_x)), 3, 1, 1, 1),
        ],
        sums,
        last=True,
    )
    mine, sums = after((mine, sums))
    moe_out, input_grad = (
        (mine[:, k : k + width] + back[:, k : k + width].astype(jnp.float32)).astype(back.dtype)
        for k in (0, width)
    )
    return (moe_out, input_grad, *sums)


def project_in(received, w_gate, w_up):
    gate = jnp.einsum("sjcd,jdf->sjcf", received, w_gate, preferred_element_type=jnp.float32)
    up = jnp.einsum("sjcd,jdf->sjcf", received, w_up, preferred_element_type=jnp.float32)
    return (gate, up)


def exchanged(tokens, expert_ids, route_weight, cotangent, w_gate, w_up, w_down):
    tok_rows, width = tokens.shape
    group = lax.axis_size("expert")
    local_exp = w_gate.shape[0]
    flat_ids = expert_ids.reshape(-1)
    onehot = (flat_ids[:, None] == jnp.arange(EXPERTS, dtype=jnp.int32)[None, :]).astype(jnp.int32)
    slot = jnp.sum((jnp.cumsum(onehot, axis=0) - onehot) * onehot, axis=1)
    target = flat_ids * CAP + slot
    token_pair = jnp.broadcast_to(tokens[:, None, :], (tok_rows, 2, width)).reshape(
        2 * tok_rows, width
    )
    outgoing = jnp.zeros((EXPERTS * CAP, width), jnp.bfloat16).at[target].set(token_pair)
    outgoing = outgoing.reshape(group, local_exp, CAP, width)
    received = lax.all_to_all(outgoing, "expert", split_axis=0, concat_axis=0, tiled=True)
    gate, up = project_in(received, w_gate, w_up)
    sig = jax.nn.sigmoid(gate)
    hidden = (gate * sig * up).astype(jnp.bfloat16)
    expert_out = jnp.einsum(
        "sjcf,jfd->sjcd", hidden, w_down, preferred_element_type=jnp.float32
    ).astype(jnp.bfloat16)
    returned = lax.all_to_all(
        expert_out, "expert", split_axis=0, concat_axis=0, tiled=True
    ).reshape(EXPERTS * CAP, width)
    picked = returned[target].reshape(tok_rows, 2, width).astype(jnp.float32)
    moe_out = jnp.sum(route_weight[:, :, None] * picked, axis=1).astype(jnp.bfloat16)
    cot_pair = jnp.broadcast_to(cotangent[:, None, :], (tok_rows, 2, width)).reshape(
        2 * tok_rows, width
    )
    scaled = (route_weight.reshape(-1)[:, None] * cot_pair.astype(jnp.float32)).astype(jnp.bfloat16)
    grad_out = jnp.zeros((EXPERTS * CAP, width), jnp.bfloat16).at[target].set(scaled)
    grad_out = grad_out.reshape(group, local_exp, CAP, width)
    drows = lax.all_to_all(grad_out, "expert", split_axis=0, concat_axis=0, tiled=True)
    dh = jnp.einsum("sjcd,jfd->sjcf", drows, w_down, preferred_element_type=jnp.float32)
    dgate = (dh * up * sig * (1.0 + gate * (1.0 - sig))).astype(jnp.bfloat16)
    dup = (dh * gate * sig).astype(jnp.bfloat16)
    dx_rows = jnp.einsum("sjcf,jdf->sjcd", dgate, w_gate, preferred_element_type=jnp.float32)
    dx_rows = (
        dx_rows + jnp.einsum("sjcf,jdf->sjcd", dup, w_up, preferred_element_type=jnp.float32)
    ).astype(jnp.bfloat16)
    dx_back = lax.all_to_all(dx_rows, "expert", split_axis=0, concat_axis=0, tiled=True).reshape(
        EXPERTS * CAP, width
    )
    input_grad = jnp.sum(
        dx_back[target].reshape(tok_rows, 2, width).astype(jnp.float32), axis=1
    ).astype(jnp.bfloat16)
    full_gate = jnp.einsum("sjcd,sjcf->jdf", received, dgate, preferred_element_type=jnp.float32)
    full_up = jnp.einsum("sjcd,sjcf->jdf", received, dup, preferred_element_type=jnp.float32)
    full_down = jnp.einsum("sjcf,sjcd->jfd", hidden, drows, preferred_element_type=jnp.float32)
    grads = [
        lax.psum_scatter(g, "dp", scatter_dimension=1, tiled=True)
        for g in (full_gate, full_up, full_down)
    ]
    return (moe_out, input_grad, *grads)


def solution(mesh):
    placed = (
        P(("dp", "expert"), None),
        P(("dp", "expert"), None),
        P(("dp", "expert"), None),
        P(("dp", "expert"), None),
        P("expert", None, None),
        P("expert", None, None),
        P("expert", None, None),
    )
    small = mesh.shape["dp"] == 8 and mesh.shape["expert"] == 4
    return jax.shard_map(
        gathered if small else exchanged,
        mesh=mesh,
        in_specs=placed,
        out_specs=(
            P(("dp", "expert"), None),
            P(("dp", "expert"), None),
            P("expert", "dp", None),
            P("expert", "dp", None),
            P("expert", "dp", None),
        ),
        check_vma=False,
    )
```

```python
import functools

import jax
import jax.numpy as jnp
from jax import lax
from jax.experimental import pallas as pl
from jax.experimental.pallas import tpu as pltpu
from jax.sharding import PartitionSpec as P

EXPERTS = 32
CAP = 24
VMEM_LIMIT = 24 * 1024 * 1024
SMALL_VMEM = 4 * 1024 * 1024
RING = 5


def route_kernel(ids_ref, rw_ref, out_ref):
    toks = ids_ref.shape[1]
    ids0, ids1 = ids_ref[0:1, :], ids_ref[1:2, :]
    expert = lax.broadcasted_iota(jnp.int32, (EXPERTS, toks), 0)
    hot0 = (expert == ids0).astype(jnp.float32)
    hot1 = (expert == ids1).astype(jnp.float32)
    row = lax.broadcasted_iota(jnp.int32, (toks, toks), 0)
    col = lax.broadcasted_iota(jnp.int32, (toks, toks), 1)
    earlier = (row < col).astype(jnp.bfloat16)
    before = jnp.dot(
        (hot0 + hot1).astype(jnp.bfloat16), earlier, preferred_element_type=jnp.float32
    )
    slot0 = jnp.sum(before * hot0, axis=0, keepdims=True)
    slot1 = jnp.sum(before * hot1, axis=0, keepdims=True)
    out_ref[0:1, :] = ids0.astype(jnp.float32) * CAP + slot0
    out_ref[1:2, :] = ids1.astype(jnp.float32) * CAP + slot1
    out_ref[2:4, :] = rw_ref[...]


def route(expert_ids, route_weight):
    toks = expert_ids.shape[0]
    return pl.pallas_call(
        route_kernel,
        out_shape=jax.ShapeDtypeStruct((4, toks), jnp.float32),
        compiler_params=pltpu.CompilerParams(vmem_limit_bytes=SMALL_VMEM),
    )(expert_ids.T, route_weight.T)


SMALL = pltpu.CompilerParams(vmem_limit_bytes=SMALL_VMEM)
FREE = pl.CostEstimate(flops=1, bytes_accessed=1, transcendentals=0)
VMEM = pl.BlockSpec(memory_space=pltpu.VMEM)
ANY = pl.BlockSpec(memory_space=pl.ANY)


def position():
    return lax.axis_index("dp"), lax.axis_index("expert")


def is_inner():
    z = position()[0] // 2
    return (z == 1) | (z == 2)


def join(a, b):
    def kernel(a_ref, b_ref, out_ref):
        out_ref[: a.shape[0]] = a_ref[...]
        out_ref[a.shape[0] :] = b_ref[...]

    return pl.pallas_call(
        kernel,
        in_specs=[VMEM] * 2,
        out_specs=VMEM,
        out_shape=jax.ShapeDtypeStruct((2 * a.shape[0],) + a.shape[1:], a.dtype),
        compiler_params=SMALL,
    )(a, b)


def pack(by, bx, block, at_ends=None):
    rows, width = block.shape[0], block.shape[1] // 2
    half = rows // 2
    choices = [block] if at_ends is None else [block, at_ends]

    def kernel(by_ref, bx_ref, *refs):
        block_refs, (px_ref, py_ref, sem) = refs[:-3], refs[-3:]
        copies = []
        for out_ref, ref, lane in ((px_ref, by_ref, width), (py_ref, bx_ref, 0)):
            for k in range(2):
                src = ref.at[pl.ds(k * half, half), pl.ds(lane, width)]
                copies.append((src, out_ref.at[pl.ds(rows, half), pl.ds(k * width, width)]))
        copies = [pltpu.make_async_copy(src, dst, sem.at[k]) for k, (src, dst) in enumerate(copies)]

        def tops(block_ref):
            return [
                pltpu.make_async_copy(block_ref, out_ref.at[pl.ds(0, rows)], sem.at[4 + k])
                for k, out_ref in enumerate((px_ref, py_ref))
            ]

        if len(block_refs) == 1:
            for c in tops(block_refs[0]):
                c.start()
        else:
            inner = is_inner()

            @pl.when(inner)
            def _():
                for c in tops(block_refs[0]):
                    c.start()

            @pl.when(jnp.logical_not(inner))
            def _():
                for c in tops(block_refs[1]):
                    c.start()

        for c in copies:
            c.start()
        for c in copies + tops(block_refs[0]):
            c.wait()

    return pl.pallas_call(
        kernel,
        in_specs=[ANY] * (2 + len(choices)),
        out_specs=[VMEM] * 2,
        out_shape=[pltpu.VMEM((rows + half, 2 * width), block.dtype)] * 2,
        scratch_shapes=[pltpu.SemaphoreType.DMA((6,))],
        compiler_params=SMALL,
    )(by, bx, *choices)


def beside(left, right):
    rows, width = left.shape

    def kernel(left_ref, right_ref, out_ref, sem):
        copies = [
            pltpu.make_async_copy(ref, out_ref.at[:, pl.ds(k * width, width)], sem.at[k])
            for k, ref in enumerate((left_ref, right_ref))
        ]
        for c in copies:
            c.start()
        for c in copies:
            c.wait()

    return pl.pallas_call(
        kernel,
        in_specs=[ANY] * 2,
        out_specs=VMEM,
        out_shape=pltpu.VMEM((rows, 2 * width), left.dtype),
        scratch_shapes=[pltpu.SemaphoreType.DMA((2,))],
        compiler_params=SMALL,
        cost_estimate=FREE,
    )(*in_hbm([left, right]))


def halves(a, b):
    rows, width = a.shape[0] * 2 // 3, a.shape[1] // 2

    def kernel(a_ref, b_ref, left_ref, right_ref, sem):
        top = pl.ds(0, rows)
        left = pltpu.make_async_copy(a_ref.at[top, pl.ds(0, width)], left_ref, sem.at[0])
        right = pltpu.make_async_copy(b_ref.at[top, pl.ds(width, width)], right_ref, sem.at[1])
        left.start()
        right.start()
        left.wait()
        right.wait()

    return pl.pallas_call(
        kernel,
        in_specs=[ANY] * 2,
        out_specs=[VMEM] * 2,
        out_shape=[pltpu.VMEM((rows, width), a.dtype)] * 2,
        scratch_shapes=[pltpu.SemaphoreType.DMA((2,))],
        compiler_params=SMALL,
    )(a, b)


def core_sum(keep, got):
    def kernel(keep_ref, got_ref, mine_ref, away_ref):
        mine_ref[...] = keep_ref[0].astype(jnp.float32) + got_ref[0].astype(jnp.float32)
        away_ref[...] = (keep_ref[1].astype(jnp.float32) + got_ref[1].astype(jnp.float32)).astype(
            away_ref.dtype
        )

    shape = keep.shape[1:]
    return pl.pallas_call(
        kernel,
        in_specs=[VMEM] * 2,
        out_specs=[VMEM] * 2,
        out_shape=[jax.ShapeDtypeStruct(shape, jnp.float32), jax.ShapeDtypeStruct(shape, keep.dtype)],
        compiler_params=pltpu.CompilerParams(vmem_limit_bytes=3 * SMALL_VMEM),
    )(keep, got)


def in_hbm(arrays):
    return [pltpu.with_memory_space_constraint(a, pltpu.HBM) for a in arrays]


def in_vmem(arrays):
    return [pltpu.with_memory_space_constraint(a, pltpu.VMEM) for a in arrays]


def load(*arrays):
    count, parts = len(arrays), arrays[0].shape[0]

    def kernel(*refs):
        sem = refs[-1]
        copies = [
            pltpu.make_async_copy(refs[k].at[j], refs[count + k].at[j], sem.at[k, j])
            for j in range(parts)
            for k in range(count)
        ]
        for c in copies:
            c.start()
        for c in copies:
            c.wait()

    return pl.pallas_call(
        kernel,
        in_specs=[ANY] * count,
        out_specs=[VMEM] * count,
        out_shape=[pltpu.VMEM(a.shape, a.dtype) for a in arrays],
        scratch_shapes=[pltpu.SemaphoreType.DMA((count, parts))],
        compiler_params=SMALL,
        cost_estimate=FREE,
    )(*in_hbm(arrays))


def pick_matrix(meta, base, slots):
    toks = meta.shape[1]
    place = lax.broadcasted_iota(jnp.int32, (slots, toks), 0)
    at0 = meta[0:1, :].astype(jnp.int32) - base
    at1 = meta[1:2, :].astype(jnp.int32) - base
    hit0, hit1 = place == at0, place == at1
    hot = jnp.where(hit0 | hit1, 1.0, 0.0).astype(jnp.bfloat16)
    weight = jnp.where(hit0, meta[2:3, :], 0.0) + jnp.where(hit1, meta[3:4, :], 0.0)
    return hot, jnp.sum(weight, axis=1, keepdims=True)


def dot(a, b, dims):
    return lax.dot_general(a, b, (dims, ((), ())), preferred_element_type=jnp.float32)


NN = ((1,), (0,))
NT = ((1,), (1,))
TN = ((0,), (0,))


def rows_kernel(pieces, n_arr, places, home, first, last, meta_ref, *refs):
    blocks = len(places)
    arrays, refs = refs[:n_arr], refs[n_arr:]
    wg_ref, wu_ref, wd_ref = refs[:3]
    refs = refs[3:]
    if not first:
        gg_in, gu_in, gd_in = refs[:3]
        refs = refs[3:]
    outs = refs[:3]
    refs = refs[3:]
    if home:
        keep_ref, send_ref = refs[:2]
        refs = refs[2:]
    tok_s, x_s, d_s, h_s, sem = refs[:5]
    refs = refs[5:]
    if last:
        sums, sem_out = refs[:3], refs[3]
        refs = refs[4:]
    else:
        sums = outs
    gg_ref, gu_ref, gd_ref = sums
    if home:
        hot_s, w_s, o_s = refs

    local_exp, width, ff = wg_ref.shape
    slots = local_exp * CAP
    replica, group = position()
    inner = is_inner()
    planes = (0, 4, jnp.where(inner, 20, 16), jnp.where(inner, 16, 20))
    sources = [planes[plane] + rest for plane, rest in places]
    base = group * slots

    ring = tok_s.shape[0]

    def fetch(b):
        for k, (sr, sc), (dr, dc), (nr, nc) in pieces[b]:
            src = arrays[k].at[pl.ds(sr, nr), pl.ds(sc, nc)]
            dst = tok_s.at[b % ring, pl.ds(dr, nr), pl.ds(dc, nc)]
            pltpu.make_async_copy(src, dst, sem.at[b % ring]).start()

    for b in range(min(ring, blocks)):
        fetch(b)

    for p in range(blocks // 2):
        pair = (2 * p, 2 * p + 1)
        hots, weights = [], []
        for b in pair:
            hot, weight = pick_matrix(meta_ref[sources[b]], base, slots)
            if home:
                hot_s[b] = hot
                w_s[b] = weight
            hots.append(hot)
            weights.append(weight)
        for b in pair:
            slot = tok_s.at[b % ring]
            pltpu.make_async_copy(slot, slot, sem.at[b % ring]).wait()
        chunk = 512
        for lane in range(0, 2 * width, chunk):
            got = [dot(hots[k], tok_s[pair[k] % ring, :, lane : lane + chunk], NN) for k in range(2)]
            if lane >= width:
                got = [got[k] * weights[k] for k in range(2)]
            for j in range(local_exp):
                rows = jnp.concatenate(
                    [got[k][j * CAP : (j + 1) * CAP] for k in range(2)], axis=0
                ).astype(jnp.bfloat16)
                to = slice(2 * p * CAP, 2 * (p + 1) * CAP)
                if lane < width:
                    x_s[j, to, lane : lane + chunk] = rows
                else:
                    d_s[j, to, lane - width : lane - width + chunk] = rows
        for b in pair:
            if b + ring < blocks:
                fetch(b + ring)

    def expert(j, carry):
        x, d = x_s[j], d_s[j]
        wg, wu, wd = wg_ref[j], wu_ref[j], wd_ref[j]
        gate = dot(x, wg, NN)
        up = dot(x, wu, NN)
        dh = dot(d, wd, NT)
        sig = jax.nn.sigmoid(gate)
        act = gate * sig
        hidden = (act * up).astype(jnp.bfloat16)
        dgate = (dh * up * sig * (1.0 + gate * (1.0 - sig))).astype(jnp.bfloat16)
        dup = (dh * act).astype(jnp.bfloat16)
        rows_g = gg_ref.shape[1]
        rows_d = gd_ref.shape[1]
        xs = x_s[j, :, pl.ds(pl.multiple_of(replica * rows_g, 128), rows_g)]
        gg = dot(xs, dgate, TN)
        gu = dot(xs, dup, TN)
        h_s[...] = hidden
        per = 128 // rows_d
        hs = h_s[:, pl.ds(pl.multiple_of(replica // per * 128, 128), 128)]
        wide = dot(hs, d, TN)
        gd = wide[0:rows_d]
        for q in range(1, per):
            gd = jnp.where(replica % per == q, wide[q * rows_d : (q + 1) * rows_d], gd)
        if first:
            gg_ref[j], gu_ref[j], gd_ref[j] = gg, gu, gd
        else:
            gg_ref[j] = gg_in[j] + gg
            gu_ref[j] = gu_in[j] + gu
            gd_ref[j] = gd_in[j] + gd
        if last:
            for k in range(3):
                pltpu.make_async_copy(sums[k].at[j], outs[k].at[j], sem_out.at[k, j]).start()
        if home:
            out = dot(hidden, wd, NN)
            dx = dot(dgate, wg, NT) + dot(dup, wu, NT)
            to = pl.ds(pl.multiple_of(j * CAP, 8), CAP)
            for b in range(blocks):
                mine = slice(b * CAP, (b + 1) * CAP)
                o_s[b, to, :width] = out[mine] * w_s[b, to, :]
                o_s[b, to, width:] = dx[mine]
        return carry

    lax.fori_loop(0, local_exp, expert, 0)

    if home:
        half = blocks // 2
        for b in range(blocks):
            got = dot(hot_s[b], o_s[b].astype(jnp.bfloat16), TN).astype(jnp.bfloat16)
            if b < half:
                keep_ref[b] = got
            else:
                send_ref[b - half] = got
    if last:
        for j in range(local_exp):
            for k in range(3):
                pltpu.make_async_copy(sums[k].at[j], outs[k].at[j], sem_out.at[k, j]).wait()


def expert_rows(places, replicas, meta, parts, weights, sums, home=False, last=False):
    local_exp, width, ff = weights[0].shape
    blocks = len(parts)
    toks = meta.shape[2]
    first = sums is None
    slots = local_exp * CAP
    rows = blocks * CAP
    rows_g, rows_d = width // replicas, ff // replicas
    arrays, pieces = [], []
    for part in parts:
        mine = []
        for array, *where in part:
            found = [k for k, a in enumerate(arrays) if a is array]
            if not found:
                arrays.append(array)
            mine.append((found[0] if found else len(arrays) - 1, *where))
        pieces.append(tuple(mine))
    sum_shapes = [(local_exp, rows_g, ff), (local_exp, rows_g, ff), (local_exp, rows_d, width)]
    in_specs = [VMEM] + [ANY] * len(arrays) + [VMEM] * 3
    arrays = in_hbm(arrays)
    operands = [meta, *arrays, *in_vmem(weights)]
    aliases = {}
    if not first:
        if not last:
            aliases = {len(operands) + k: k for k in range(3)}
        in_specs += [VMEM] * 3
        operands += in_vmem(sums)
    if last:
        out_shape = [jax.ShapeDtypeStruct(s, jnp.float32) for s in sum_shapes]
        out_specs = [ANY] * 3
    else:
        out_shape = [pltpu.VMEM(s, jnp.float32) for s in sum_shapes]
        out_specs = [VMEM] * 3
    scratch = [
        pltpu.VMEM((min(blocks, RING), toks, 2 * width), jnp.bfloat16),
        pltpu.VMEM((local_exp, rows, width), jnp.bfloat16),
        pltpu.VMEM((local_exp, rows, width), jnp.bfloat16),
        pltpu.VMEM((rows, ff), jnp.bfloat16),
        pltpu.SemaphoreType.DMA((min(blocks, RING),)),
    ]
    if last:
        scratch += [pltpu.VMEM(s, jnp.float32) for s in sum_shapes]
        scratch += [pltpu.SemaphoreType.DMA((3, local_exp))]
    if home:
        out_shape += [jax.ShapeDtypeStruct((blocks // 2, toks, 2 * width), jnp.bfloat16)] * 2
        out_specs += [VMEM] * 2
        scratch += [
            pltpu.VMEM((blocks, slots, toks), jnp.bfloat16),
            pltpu.VMEM((blocks, slots, 1), jnp.float32),
            pltpu.VMEM((blocks, slots, 2 * width), jnp.float32),
        ]
    kernel = functools.partial(
        rows_kernel,
        tuple(pieces),
        len(arrays),
        tuple(places),
        home,
        first,
        last,
    )
    return pl.pallas_call(
        kernel,
        in_specs=in_specs,
        out_specs=out_specs,
        scratch_shapes=scratch,
        out_shape=out_shape,
        input_output_aliases=aliases,
        compiler_params=pltpu.CompilerParams(vmem_limit_bytes=VMEM_LIMIT),
        cost_estimate=FREE,
    )(*operands)


def gathered(tokens, expert_ids, route_weight, cotangent, w_gate, w_up, w_down):
    width = tokens.shape[1]
    local_exp = w_gate.shape[0]
    replicas, group = lax.axis_size("dp"), lax.axis_size("expert")
    axes = ("dp", "expert")
    def permute(value, move):
        pairs = []
        for dp in range(replicas):
            for ex in range(group):
                to = move(dp // 2, dp % 2, ex // 2, ex % 2)
                if to is not None:
                    tz, tx, ty, tc = to
                    pairs.append((dp * group + ex, (tz * 2 + tx) * group + ty * 2 + tc))
        return lax.ppermute(value, axes, pairs)

    over_x = lambda v: permute(v, lambda z, x, y, c: (z, 1 - x, y, c))
    over_y = lambda v: permute(v, lambda z, x, y, c: (z, x, 1 - y, c))
    over_c = lambda v: permute(v, lambda z, x, y, c: (z, x, y, 1 - c))
    near = lambda v: permute(v, lambda z, x, y, c: (z ^ 1, x, y, c))
    opposite = lambda v: permute(v, lambda z, x, y, c: (z ^ 2, x, y, c))
    mid = lambda v: permute(v, lambda z, x, y, c: (z ^ 3, x, y, c) if z in (1, 2) else None)
    outward = lambda v: permute(v, lambda z, x, y, c: (z ^ 1, x, y, c) if z in (1, 2) else None)

    own = beside(tokens, cotangent)
    toks = own.shape[0]
    half = toks // 2

    def whole(array):
        return ((array, (0, 0), (0, 0), (toks, 2 * width)),)

    def packed(px, py):
        return tuple(
            (array, (toks, k * width), (k * half, lane), (half, width))
            for array, lane in ((py, 0), (px, width))
            for k in range(2)
        )

    def split(left, right):
        return (left, (0, 0), (0, 0), (toks, width)), (right, (0, 0), (0, width), (toks, width))

    def rows(meta, blocks, sums, **kind):
        parts = [b[0] for b in blocks]
        places = [(z, c + y * 2 + x * 8) for _, z, x, c, y in blocks]
        return expert_rows(places, replicas, meta, parts, weights, sums, **kind)

    after = lax.optimization_barrier

    meta = route(expert_ids, route_weight)[None]
    meta_c = over_c(meta)
    bx0, by0, d1, m1 = over_x(own), over_y(own), near(own), mid(own)
    meta = join(meta, meta_c)
    meta_y = over_y(meta)
    weights = load(w_gate, w_up, w_down)

    by0, bx0, d1, meta_y, weights, own_late = after((by0, bx0, d1, meta_y, weights, own))
    px1, py1 = pack(by0, bx0, d1)
    x1, y1, e1, m2 = over_x(px1), over_y(py1), outward(m1), mid(d1)
    meta_home = join(meta, meta_y)
    meta_here = join(meta_home, near(meta_home))
    meta_x = over_x(meta_here)
    own_c, by0_c = over_c(own_late), over_c(by0)
    *sums, keep, send = rows(
        meta_home,
        [
            (split(tokens, cotangent), 0, 0, 0, 0),
            (whole(by0), 0, 0, 0, 1),
            (whole(own_c), 0, 0, 1, 0),
            (whole(by0_c), 0, 0, 1, 1),
        ],
        None,
        home=True,
    )

    keep, send, x1, y1, e1, m2, meta_x, sums = after((keep, send, x1, y1, e1, m2, meta_x, sums))
    px2, py2 = pack(y1, x1, m1, at_ends=e1)
    px2, py2, x1, y1, bx0, d1 = after((px2, py2, x1, y1, bx0, d1))
    x2, y2, e2 = over_x(px2), over_y(py2), outward(m2)
    meta_half = join(meta_here, meta_x)
    meta_far = opposite(meta_half)
    x1_c, y1_c, bx0_c, d1_c = over_c(x1), over_c(y1), over_c(bx0), over_c(d1)
    sums = rows(
        meta_half,
        [
            (whole(bx0), 0, 1, 0, 0),
            (whole(bx0_c), 0, 1, 1, 0),
            (whole(x1), 1, 1, 0, 0),
            (whole(x1_c), 1, 1, 1, 0),
            (whole(y1), 1, 0, 0, 1),
            (whole(y1_c), 1, 0, 1, 1),
            (packed(x1, y1), 0, 1, 0, 1),
            (packed(x1_c, y1_c), 0, 1, 1, 1),
        ],
        sums,
    )

    x2, y2, e2, meta_far, d1_c, sums = after((x2, y2, e2, meta_far, d1_c, sums))
    px3, py3 = pack(y2, x2, m2, at_ends=e2)
    px3, py3, x2, y2, px2, send = after((px3, py3, x2, y2, px2, send))
    x3, y3 = over_x(px3), over_y(py3)
    meta_all = join(meta_half, meta_far)
    x2_c, y2_c, got = over_c(x2), over_c(y2), over_c(send)
    px2_c, px3_c = over_c(px2), over_c(px3)
    mine, away = core_sum(keep, got)
    sums = rows(
        meta_all,
        [
            (whole(d1), 1, 0, 0, 0),
            (whole(d1_c), 1, 0, 1, 0),
            (whole(x2), 2, 1, 0, 0),
            (whole(x2_c), 2, 1, 1, 0),
            (whole(y2), 2, 0, 0, 1),
            (whole(y2_c), 2, 0, 1, 1),
            (packed(x2, y2), 1, 1, 0, 1),
            (packed(x2_c, y2_c), 1, 1, 1, 1),
        ],
        sums,
    )

    x3, y3, px2_c, px3_c, away, sums = after((x3, y3, px2_c, px3_c, away, sums))
    left, right = halves(x3, y3)
    by_y, by_x = over_y(left), over_x(right)
    back = over_y(away)
    x3_c, y3_c = over_c(x3), over_c(y3)
    sums = rows(
        meta_all,
        [
            (whole(px2), 2, 0, 0, 0),
            (whole(px2_c), 2, 0, 1, 0),
            (whole(px3), 3, 0, 0, 0),
            (whole(px3_c), 3, 0, 1, 0),
            (whole(x3), 3, 1, 0, 0),
            (whole(y3), 3, 0, 0, 1),
        ],
        sums,
    )

    by_y, by_x, sums = after((by_y, by_x, sums))
    sums = rows(
        meta_all,
        [
            (whole(x3_c), 3, 1, 1, 0),
            (whole(y3_c), 3, 0, 1, 1),
            (packed(x3, y3), 2, 1, 0, 1),
            (packed(x3_c, y3_c), 2, 1, 1, 1),
            (split(by_y, by_x), 3, 1, 0, 1),
            (split(over_c(by_y), over_c(by_x)), 3, 1, 1, 1),
        ],
        sums,
        last=True,
    )
    mine, sums = after((mine, sums))
    moe_out, input_grad = (
        (mine[:, k : k + width] + back[:, k : k + width].astype(jnp.float32)).astype(back.dtype)
        for k in (0, width)
    )
    return (moe_out, input_grad, *sums)


def project_in(received, w_gate, w_up):
    gate = jnp.einsum("sjcd,jdf->sjcf", received, w_gate, preferred_element_type=jnp.float32)
    up = jnp.einsum("sjcd,jdf->sjcf", received, w_up, preferred_element_type=jnp.float32)
    return (gate, up)


def exchanged(tokens, expert_ids, route_weight, cotangent, w_gate, w_up, w_down):
    tok_rows, width = tokens.shape
    group = lax.axis_size("expert")
    local_exp = w_gate.shape[0]
    flat_ids = expert_ids.reshape(-1)
    onehot = (flat_ids[:, None] == jnp.arange(EXPERTS, dtype=jnp.int32)[None, :]).astype(jnp.int32)
    slot = jnp.sum((jnp.cumsum(onehot, axis=0) - onehot) * onehot, axis=1)
    target = flat_ids * CAP + slot
    token_pair = jnp.broadcast_to(tokens[:, None, :], (tok_rows, 2, width)).reshape(
        2 * tok_rows, width
    )
    outgoing = jnp.zeros((EXPERTS * CAP, width), jnp.bfloat16).at[target].set(token_pair)
    outgoing = outgoing.reshape(group, local_exp, CAP, width)
    received = lax.all_to_all(outgoing, "expert", split_axis=0, concat_axis=0, tiled=True)
    gate, up = project_in(received, w_gate, w_up)
    sig = jax.nn.sigmoid(gate)
    hidden = (gate * sig * up).astype(jnp.bfloat16)
    expert_out = jnp.einsum(
        "sjcf,jfd->sjcd", hidden, w_down, preferred_element_type=jnp.float32
    ).astype(jnp.bfloat16)
    returned = lax.all_to_all(
        expert_out, "expert", split_axis=0, concat_axis=0, tiled=True
    ).reshape(EXPERTS * CAP, width)
    picked = returned[target].reshape(tok_rows, 2, width).astype(jnp.float32)
    moe_out = jnp.sum(route_weight[:, :, None] * picked, axis=1).astype(jnp.bfloat16)
    cot_pair = jnp.broadcast_to(cotangent[:, None, :], (tok_rows, 2, width)).reshape(
        2 * tok_rows, width
    )
    scaled = (route_weight.reshape(-1)[:, None] * cot_pair.astype(jnp.float32)).astype(jnp.bfloat16)
    grad_out = jnp.zeros((EXPERTS * CAP, width), jnp.bfloat16).at[target].set(scaled)
    grad_out = grad_out.reshape(group, local_exp, CAP, width)
    drows = lax.all_to_all(grad_out, "expert", split_axis=0, concat_axis=0, tiled=True)
    dh = jnp.einsum("sjcd,jfd->sjcf", drows, w_down, preferred_element_type=jnp.float32)
    dgate = (dh * up * sig * (1.0 + gate * (1.0 - sig))).astype(jnp.bfloat16)
    dup = (dh * gate * sig).astype(jnp.bfloat16)
    dx_rows = jnp.einsum("sjcf,jdf->sjcd", dgate, w_gate, preferred_element_type=jnp.float32)
    dx_rows = (
        dx_rows + jnp.einsum("sjcf,jdf->sjcd", dup, w_up, preferred_element_type=jnp.float32)
    ).astype(jnp.bfloat16)
    dx_back = lax.all_to_all(dx_rows, "expert", split_axis=0, concat_axis=0, tiled=True).reshape(
        EXPERTS * CAP, width
    )
    input_grad = jnp.sum(
        dx_back[target].reshape(tok_rows, 2, width).astype(jnp.float32), axis=1
    ).astype(jnp.bfloat16)
    full_gate = jnp.einsum("sjcd,sjcf->jdf", received, dgate, preferred_element_type=jnp.float32)
    full_up = jnp.einsum("sjcd,sjcf->jdf", received, dup, preferred_element_type=jnp.float32)
    full_down = jnp.einsum("sjcf,sjcd->jfd", hidden, drows, preferred_element_type=jnp.float32)
    grads = [
        lax.psum_scatter(g, "dp", scatter_dimension=1, tiled=True)
        for g in (full_gate, full_up, full_down)
    ]
    return (moe_out, input_grad, *grads)


def solution(mesh):
    placed = (
        P(("dp", "expert"), None),
        P(("dp", "expert"), None),
        P(("dp", "expert"), None),
        P(("dp", "expert"), None),
        P("expert", None, None),
        P("expert", None, None),
        P("expert", None, None),
    )
    small = mesh.shape["dp"] == 8 and mesh.shape["expert"] == 4
    return jax.shard_map(
        gathered if small else exchanged,
        mesh=mesh,
        in_specs=placed,
        out_specs=(
            P(("dp", "expert"), None),
            P(("dp", "expert"), None),
            P("expert", "dp", None),
            P("expert", "dp", None),
            P("expert", "dp", None),
        ),
        check_vma=False,
    )
```

```python
import functools

import jax
import jax.numpy as jnp
from jax import lax
from jax.experimental import pallas as pl
from jax.experimental.pallas import tpu as pltpu
from jax.sharding import PartitionSpec as P

EXPERTS = 32
CAP = 24
VMEM_LIMIT = 22 * 1024 * 1024
SMALL_VMEM = 4 * 1024 * 1024
RING = 4


def route_kernel(ids_ref, rw_ref, out_ref):
    toks = ids_ref.shape[1]
    ids0, ids1 = ids_ref[0:1, :], ids_ref[1:2, :]
    expert = lax.broadcasted_iota(jnp.int32, (EXPERTS, toks), 0)
    hot0 = (expert == ids0).astype(jnp.float32)
    hot1 = (expert == ids1).astype(jnp.float32)
    row = lax.broadcasted_iota(jnp.int32, (toks, toks), 0)
    col = lax.broadcasted_iota(jnp.int32, (toks, toks), 1)
    earlier = (row < col).astype(jnp.bfloat16)
    before = jnp.dot(
        (hot0 + hot1).astype(jnp.bfloat16), earlier, preferred_element_type=jnp.float32
    )
    slot0 = jnp.sum(before * hot0, axis=0, keepdims=True)
    slot1 = jnp.sum(before * hot1, axis=0, keepdims=True)
    out_ref[0:1, :] = ids0.astype(jnp.float32) * CAP + slot0
    out_ref[1:2, :] = ids1.astype(jnp.float32) * CAP + slot1
    out_ref[2:4, :] = rw_ref[...]


def route(expert_ids, route_weight):
    toks = expert_ids.shape[0]
    return pl.pallas_call(
        route_kernel,
        out_shape=jax.ShapeDtypeStruct((4, toks), jnp.float32),
        compiler_params=pltpu.CompilerParams(vmem_limit_bytes=SMALL_VMEM),
    )(expert_ids.T, route_weight.T)


SMALL = pltpu.CompilerParams(vmem_limit_bytes=SMALL_VMEM)
FREE = pl.CostEstimate(flops=1, bytes_accessed=1, transcendentals=0)
VMEM = pl.BlockSpec(memory_space=pltpu.VMEM)
ANY = pl.BlockSpec(memory_space=pl.ANY)


def position():
    return lax.axis_index("dp"), lax.axis_index("expert")


def is_inner():
    z = position()[0] // 2
    return (z == 1) | (z == 2)


def join(a, b):
    def kernel(a_ref, b_ref, out_ref):
        out_ref[: a.shape[0]] = a_ref[...]
        out_ref[a.shape[0] :] = b_ref[...]

    return pl.pallas_call(
        kernel,
        in_specs=[VMEM] * 2,
        out_specs=VMEM,
        out_shape=jax.ShapeDtypeStruct((2 * a.shape[0],) + a.shape[1:], a.dtype),
        compiler_params=SMALL,
    )(a, b)


def pack(by, bx, block, at_ends=None):
    rows, width = block.shape[0], block.shape[1] // 2
    half = rows // 2
    choices = [block] if at_ends is None else [block, at_ends]

    def kernel(by_ref, bx_ref, *refs):
        block_refs, (px_ref, py_ref, sem) = refs[:-3], refs[-3:]
        copies = []
        for out_ref, ref, lane in ((px_ref, by_ref, width), (py_ref, bx_ref, 0)):
            for k in range(2):
                src = ref.at[pl.ds(k * half, half), pl.ds(lane, width)]
                copies.append((src, out_ref.at[pl.ds(rows, half), pl.ds(k * width, width)]))
        copies = [pltpu.make_async_copy(src, dst, sem.at[k]) for k, (src, dst) in enumerate(copies)]

        def tops(block_ref):
            return [
                pltpu.make_async_copy(block_ref, out_ref.at[pl.ds(0, rows)], sem.at[4 + k])
                for k, out_ref in enumerate((px_ref, py_ref))
            ]

        if len(block_refs) == 1:
            for c in tops(block_refs[0]):
                c.start()
        else:
            inner = is_inner()

            @pl.when(inner)
            def _():
                for c in tops(block_refs[0]):
                    c.start()

            @pl.when(jnp.logical_not(inner))
            def _():
                for c in tops(block_refs[1]):
                    c.start()

        for c in copies:
            c.start()
        for c in copies + tops(block_refs[0]):
            c.wait()

    return pl.pallas_call(
        kernel,
        in_specs=[ANY] * (2 + len(choices)),
        out_specs=[VMEM] * 2,
        out_shape=[pltpu.VMEM((rows + half, 2 * width), block.dtype)] * 2,
        scratch_shapes=[pltpu.SemaphoreType.DMA((6,))],
        compiler_params=SMALL,
    )(by, bx, *choices)


def beside(left, right):
    rows, width = left.shape

    def kernel(left_ref, right_ref, out_ref, sem):
        copies = [
            pltpu.make_async_copy(ref, out_ref.at[:, pl.ds(k * width, width)], sem.at[k])
            for k, ref in enumerate((left_ref, right_ref))
        ]
        for c in copies:
            c.start()
        for c in copies:
            c.wait()

    return pl.pallas_call(
        kernel,
        in_specs=[ANY] * 2,
        out_specs=VMEM,
        out_shape=pltpu.VMEM((rows, 2 * width), left.dtype),
        scratch_shapes=[pltpu.SemaphoreType.DMA((2,))],
        compiler_params=SMALL,
        cost_estimate=FREE,
    )(*in_hbm([left, right]))


def halves(a, b):
    rows, width = a.shape[0] * 2 // 3, a.shape[1] // 2

    def kernel(a_ref, b_ref, left_ref, right_ref, sem):
        top = pl.ds(0, rows)
        left = pltpu.make_async_copy(a_ref.at[top, pl.ds(0, width)], left_ref, sem.at[0])
        right = pltpu.make_async_copy(b_ref.at[top, pl.ds(width, width)], right_ref, sem.at[1])
        left.start()
        right.start()
        left.wait()
        right.wait()

    return pl.pallas_call(
        kernel,
        in_specs=[ANY] * 2,
        out_specs=[VMEM] * 2,
        out_shape=[pltpu.VMEM((rows, width), a.dtype)] * 2,
        scratch_shapes=[pltpu.SemaphoreType.DMA((2,))],
        compiler_params=SMALL,
    )(a, b)


def core_sum(keep, got):
    def kernel(keep_ref, got_ref, mine_ref, away_ref):
        mine_ref[...] = keep_ref[0].astype(jnp.float32) + got_ref[0].astype(jnp.float32)
        away_ref[...] = (keep_ref[1].astype(jnp.float32) + got_ref[1].astype(jnp.float32)).astype(
            away_ref.dtype
        )

    shape = keep.shape[1:]
    return pl.pallas_call(
        kernel,
        in_specs=[VMEM] * 2,
        out_specs=[VMEM] * 2,
        out_shape=[jax.ShapeDtypeStruct(shape, jnp.float32), jax.ShapeDtypeStruct(shape, keep.dtype)],
        compiler_params=pltpu.CompilerParams(vmem_limit_bytes=3 * SMALL_VMEM),
    )(keep, got)


def in_hbm(arrays):
    return [pltpu.with_memory_space_constraint(a, pltpu.HBM) for a in arrays]


def in_vmem(arrays):
    return [pltpu.with_memory_space_constraint(a, pltpu.VMEM) for a in arrays]


def load(*arrays):
    count, parts = len(arrays), arrays[0].shape[0]

    def kernel(*refs):
        sem = refs[-1]
        copies = [
            pltpu.make_async_copy(refs[k].at[j], refs[count + k].at[j], sem.at[k, j])
            for j in range(parts)
            for k in range(count)
        ]
        for c in copies:
            c.start()
        for c in copies:
            c.wait()

    return pl.pallas_call(
        kernel,
        in_specs=[ANY] * count,
        out_specs=[VMEM] * count,
        out_shape=[pltpu.VMEM(a.shape, a.dtype) for a in arrays],
        scratch_shapes=[pltpu.SemaphoreType.DMA((count, parts))],
        compiler_params=SMALL,
        cost_estimate=FREE,
    )(*in_hbm(arrays))


def pick_matrix(meta, base, slots):
    toks = meta.shape[1]
    place = lax.broadcasted_iota(jnp.int32, (slots, toks), 0)
    at0 = meta[0:1, :].astype(jnp.int32) - base
    at1 = meta[1:2, :].astype(jnp.int32) - base
    hit0, hit1 = place == at0, place == at1
    hot = jnp.where(hit0 | hit1, 1.0, 0.0).astype(jnp.bfloat16)
    weight = jnp.where(hit0, meta[2:3, :], 0.0) + jnp.where(hit1, meta[3:4, :], 0.0)
    return hot, jnp.sum(weight, axis=1, keepdims=True)


def dot(a, b, dims):
    return lax.dot_general(a, b, (dims, ((), ())), preferred_element_type=jnp.float32)


NN = ((1,), (0,))
NT = ((1,), (1,))
TN = ((0,), (0,))


def rows_kernel(pieces, n_arr, places, home, first, last, meta_ref, *refs):
    blocks = len(places)
    arrays, refs = refs[:n_arr], refs[n_arr:]
    wg_ref, wu_ref, wd_ref = refs[:3]
    refs = refs[3:]
    if not first:
        gg_in, gu_in, gd_in = refs[:3]
        refs = refs[3:]
    outs = refs[:3]
    refs = refs[3:]
    if home:
        keep_ref, send_ref = refs[:2]
        refs = refs[2:]
    tok_s, x_s, d_s, h_s, sem = refs[:5]
    refs = refs[5:]
    if last:
        sums, sem_out = refs[:3], refs[3]
        refs = refs[4:]
    else:
        sums = outs
    gg_ref, gu_ref, gd_ref = sums
    if home:
        hot_s, w_s, o_s = refs

    local_exp, width, ff = wg_ref.shape
    slots = local_exp * CAP
    replica, group = position()
    inner = is_inner()
    planes = (0, 4, jnp.where(inner, 20, 16), jnp.where(inner, 16, 20))
    sources = [planes[plane] + rest for plane, rest in places]
    base = group * slots

    ring = tok_s.shape[0]

    def fetch(b):
        for k, (sr, sc), (dr, dc), (nr, nc) in pieces[b]:
            src = arrays[k].at[pl.ds(sr, nr), pl.ds(sc, nc)]
            dst = tok_s.at[b % ring, pl.ds(dr, nr), pl.ds(dc, nc)]
            pltpu.make_async_copy(src, dst, sem.at[b % ring]).start()

    for b in range(min(ring, blocks)):
        fetch(b)

    for p in range(blocks // 2):
        pair = (2 * p, 2 * p + 1)
        hots, weights = [], []
        for b in pair:
            hot, weight = pick_matrix(meta_ref[sources[b]], base, slots)
            if home:
                hot_s[b] = hot
                w_s[b] = weight
            hots.append(hot)
            weights.append(weight)
        for b in pair:
            slot = tok_s.at[b % ring]
            pltpu.make_async_copy(slot, slot, sem.at[b % ring]).wait()
        chunk = 512
        for lane in range(0, 2 * width, chunk):
            got = [dot(hots[k], tok_s[pair[k] % ring, :, lane : lane + chunk], NN) for k in range(2)]
            if lane >= width:
                got = [got[k] * weights[k] for k in range(2)]
            for j in range(local_exp):
                rows = jnp.concatenate(
                    [got[k][j * CAP : (j + 1) * CAP] for k in range(2)], axis=0
                ).astype(jnp.bfloat16)
                to = slice(2 * p * CAP, 2 * (p + 1) * CAP)
                if lane < width:
                    x_s[j, to, lane : lane + chunk] = rows
                else:
                    d_s[j, to, lane - width : lane - width + chunk] = rows
        for b in pair:
            if b + ring < blocks:
                fetch(b + ring)

    def expert(j, carry):
        x, d = x_s[j], d_s[j]
        wg, wu, wd = wg_ref[j], wu_ref[j], wd_ref[j]
        gate = dot(x, wg, NN)
        up = dot(x, wu, NN)
        dh = dot(d, wd, NT)
        sig = jax.nn.sigmoid(gate)
        act = gate * sig
        hidden = (act * up).astype(jnp.bfloat16)
        dgate = (dh * up * sig * (1.0 + gate * (1.0 - sig))).astype(jnp.bfloat16)
        dup = (dh * act).astype(jnp.bfloat16)
        rows_g = gg_ref.shape[1]
        rows_d = gd_ref.shape[1]
        xs = x_s[j, :, pl.ds(pl.multiple_of(replica * rows_g, 128), rows_g)]
        gg = dot(xs, dgate, TN)
        gu = dot(xs, dup, TN)
        h_s[...] = hidden
        per = 128 // rows_d
        hs = h_s[:, pl.ds(pl.multiple_of(replica // per * 128, 128), 128)]
        wide = dot(hs, d, TN)
        gd = wide[0:rows_d]
        for q in range(1, per):
            gd = jnp.where(replica % per == q, wide[q * rows_d : (q + 1) * rows_d], gd)
        if first:
            gg_ref[j], gu_ref[j], gd_ref[j] = gg, gu, gd
        else:
            gg_ref[j] = gg_in[j] + gg
            gu_ref[j] = gu_in[j] + gu
            gd_ref[j] = gd_in[j] + gd
        if last:
            for k in range(3):
                pltpu.make_async_copy(sums[k].at[j], outs[k].at[j], sem_out.at[k, j]).start()
        if home:
            out = dot(hidden, wd, NN)
            dx = dot(dgate, wg, NT) + dot(dup, wu, NT)
            to = pl.ds(pl.multiple_of(j * CAP, 8), CAP)
            for b in range(blocks):
                mine = slice(b * CAP, (b + 1) * CAP)
                o_s[b, to, :width] = out[mine] * w_s[b, to, :]
                o_s[b, to, width:] = dx[mine]
        return carry

    lax.fori_loop(0, local_exp, expert, 0)

    if home:
        half = blocks // 2
        for b in range(blocks):
            got = dot(hot_s[b], o_s[b].astype(jnp.bfloat16), TN).astype(jnp.bfloat16)
            if b < half:
                keep_ref[b] = got
            else:
                send_ref[b - half] = got
    if last:
        for j in range(local_exp):
            for k in range(3):
                pltpu.make_async_copy(sums[k].at[j], outs[k].at[j], sem_out.at[k, j]).wait()


def expert_rows(places, replicas, meta, parts, weights, sums, home=False, last=False):
    local_exp, width, ff = weights[0].shape
    blocks = len(parts)
    toks = meta.shape[2]
    first = sums is None
    slots = local_exp * CAP
    rows = blocks * CAP
    ring = 2 if home else min(blocks, RING)
    rows_g, rows_d = width // replicas, ff // replicas
    arrays, pieces = [], []
    for part in parts:
        mine = []
        for array, *where in part:
            found = [k for k, a in enumerate(arrays) if a is array]
            if not found:
                arrays.append(array)
            mine.append((found[0] if found else len(arrays) - 1, *where))
        pieces.append(tuple(mine))
    sum_shapes = [(local_exp, rows_g, ff), (local_exp, rows_g, ff), (local_exp, rows_d, width)]
    in_specs = [VMEM] + [ANY] * len(arrays) + [VMEM] * 3
    arrays = in_hbm(arrays)
    operands = [meta, *arrays, *in_vmem(weights)]
    aliases = {}
    if not first:
        if not last:
            aliases = {len(operands) + k: k for k in range(3)}
        in_specs += [VMEM] * 3
        operands += in_vmem(sums)
    if last:
        out_shape = [jax.ShapeDtypeStruct(s, jnp.float32) for s in sum_shapes]
        out_specs = [ANY] * 3
    else:
        out_shape = [pltpu.VMEM(s, jnp.float32) for s in sum_shapes]
        out_specs = [VMEM] * 3
    scratch = [
        pltpu.VMEM((ring, toks, 2 * width), jnp.bfloat16),
        pltpu.VMEM((local_exp, rows, width), jnp.bfloat16),
        pltpu.VMEM((local_exp, rows, width), jnp.bfloat16),
        pltpu.VMEM((rows, ff), jnp.bfloat16),
        pltpu.SemaphoreType.DMA((ring,)),
    ]
    if last:
        scratch += [pltpu.VMEM(s, jnp.float32) for s in sum_shapes]
        scratch += [pltpu.SemaphoreType.DMA((3, local_exp))]
    if home:
        out_shape += [jax.ShapeDtypeStruct((blocks // 2, toks, 2 * width), jnp.bfloat16)] * 2
        out_specs += [VMEM] * 2
        scratch += [
            pltpu.VMEM((blocks, slots, toks), jnp.bfloat16),
            pltpu.VMEM((blocks, slots, 1), jnp.float32),
            pltpu.VMEM((blocks, slots, 2 * width), jnp.float32),
        ]
    kernel = functools.partial(
        rows_kernel,
        tuple(pieces),
        len(arrays),
        tuple(places),
        home,
        first,
        last,
    )
    return pl.pallas_call(
        kernel,
        in_specs=in_specs,
        out_specs=out_specs,
        scratch_shapes=scratch,
        out_shape=out_shape,
        input_output_aliases=aliases,
        compiler_params=pltpu.CompilerParams(vmem_limit_bytes=VMEM_LIMIT),
        cost_estimate=FREE,
    )(*operands)


def gathered(tokens, expert_ids, route_weight, cotangent, w_gate, w_up, w_down):
    width = tokens.shape[1]
    local_exp = w_gate.shape[0]
    replicas, group = lax.axis_size("dp"), lax.axis_size("expert")
    axes = ("dp", "expert")
    def permute(value, move):
        pairs = []
        for dp in range(replicas):
            for ex in range(group):
                to = move(dp // 2, dp % 2, ex // 2, ex % 2)
                if to is not None:
                    tz, tx, ty, tc = to
                    pairs.append((dp * group + ex, (tz * 2 + tx) * group + ty * 2 + tc))
        return lax.ppermute(value, axes, pairs)

    over_x = lambda v: permute(v, lambda z, x, y, c: (z, 1 - x, y, c))
    over_y = lambda v: permute(v, lambda z, x, y, c: (z, x, 1 - y, c))
    over_c = lambda v: permute(v, lambda z, x, y, c: (z, x, y, 1 - c))
    near = lambda v: permute(v, lambda z, x, y, c: (z ^ 1, x, y, c))
    opposite = lambda v: permute(v, lambda z, x, y, c: (z ^ 2, x, y, c))
    mid = lambda v: permute(v, lambda z, x, y, c: (z ^ 3, x, y, c) if z in (1, 2) else None)
    outward = lambda v: permute(v, lambda z, x, y, c: (z ^ 1, x, y, c) if z in (1, 2) else None)

    own = beside(tokens, cotangent)
    toks = own.shape[0]
    half = toks // 2

    def whole(array):
        return ((array, (0, 0), (0, 0), (toks, 2 * width)),)

    def packed(px, py):
        return tuple(
            (array, (toks, k * width), (k * half, lane), (half, width))
            for array, lane in ((py, 0), (px, width))
            for k in range(2)
        )

    def split(left, right):
        return (left, (0, 0), (0, 0), (toks, width)), (right, (0, 0), (0, width), (toks, width))

    def rows(meta, blocks, sums, **kind):
        parts = [b[0] for b in blocks]
        places = [(z, c + y * 2 + x * 8) for _, z, x, c, y in blocks]
        return expert_rows(places, replicas, meta, parts, weights, sums, **kind)

    after = lax.optimization_barrier

    meta = route(expert_ids, route_weight)[None]
    meta_c = over_c(meta)
    bx0, by0, d1, m1 = over_x(own), over_y(own), near(own), mid(own)
    meta = join(meta, meta_c)
    meta_y = over_y(meta)
    weights = load(w_gate, w_up, w_down)

    by0, bx0, d1, meta_y, weights, own_late = after((by0, bx0, d1, meta_y, weights, own))
    px1, py1 = pack(by0, bx0, d1)
    x1, y1, e1, m2 = over_x(px1), over_y(py1), outward(m1), mid(d1)
    meta_home = join(meta, meta_y)
    meta_here = join(meta_home, near(meta_home))
    meta_x = over_x(meta_here)
    own_c, by0_c = over_c(own_late), over_c(by0)
    *sums, keep, send = rows(
        meta_home,
        [
            (split(tokens, cotangent), 0, 0, 0, 0),
            (whole(by0), 0, 0, 0, 1),
            (whole(own_c), 0, 0, 1, 0),
            (whole(by0_c), 0, 0, 1, 1),
        ],
        None,
        home=True,
    )

    keep, send, x1, y1, e1, m2, meta_x, sums = after((keep, send, x1, y1, e1, m2, meta_x, sums))
    px2, py2 = pack(y1, x1, m1, at_ends=e1)
    px2, py2, x1, y1, bx0, d1 = after((px2, py2, x1, y1, bx0, d1))
    x2, y2, e2 = over_x(px2), over_y(py2), outward(m2)
    meta_half = join(meta_here, meta_x)
    meta_far = opposite(meta_half)
    x1_c, y1_c, bx0_c, d1_c = over_c(x1), over_c(y1), over_c(bx0), over_c(d1)
    sums = rows(
        meta_half,
        [
            (whole(bx0), 0, 1, 0, 0),
            (whole(bx0_c), 0, 1, 1, 0),
            (whole(x1), 1, 1, 0, 0),
            (whole(x1_c), 1, 1, 1, 0),
            (whole(y1), 1, 0, 0, 1),
            (whole(y1_c), 1, 0, 1, 1),
            (packed(x1, y1), 0, 1, 0, 1),
            (packed(x1_c, y1_c), 0, 1, 1, 1),
        ],
        sums,
    )

    x2, y2, e2, meta_far, d1_c, sums = after((x2, y2, e2, meta_far, d1_c, sums))
    px3, py3 = pack(y2, x2, m2, at_ends=e2)
    px3, py3, x2, y2, px2, send = after((px3, py3, x2, y2, px2, send))
    x3, y3 = over_x(px3), over_y(py3)
    meta_all = join(meta_half, meta_far)
    x2_c, y2_c, got = over_c(x2), over_c(y2), over_c(send)
    px2_c, px3_c = over_c(px2), over_c(px3)
    mine, away = core_sum(keep, got)
    sums = rows(
        meta_all,
        [
            (whole(d1), 1, 0, 0, 0),
            (whole(d1_c), 1, 0, 1, 0),
            (whole(x2), 2, 1, 0, 0),
            (whole(x2_c), 2, 1, 1, 0),
            (whole(y2), 2, 0, 0, 1),
            (whole(y2_c), 2, 0, 1, 1),
            (packed(x2, y2), 1, 1, 0, 1),
            (packed(x2_c, y2_c), 1, 1, 1, 1),
        ],
        sums,
    )

    x3, y3, px2_c, px3_c, away, sums = after((x3, y3, px2_c, px3_c, away, sums))
    left, right = halves(x3, y3)
    by_y, by_x = over_y(left), over_x(right)
    back = over_y(away)
    x3_c, y3_c = over_c(x3), over_c(y3)
    sums = rows(
        meta_all,
        [
            (whole(px2), 2, 0, 0, 0),
            (whole(px2_c), 2, 0, 1, 0),
            (whole(px3), 3, 0, 0, 0),
            (whole(px3_c), 3, 0, 1, 0),
            (whole(x3), 3, 1, 0, 0),
            (whole(y3), 3, 0, 0, 1),
        ],
        sums,
    )

    by_y, by_x, sums = after((by_y, by_x, sums))
    sums = rows(
        meta_all,
        [
            (whole(x3_c), 3, 1, 1, 0),
            (whole(y3_c), 3, 0, 1, 1),
            (packed(x3, y3), 2, 1, 0, 1),
            (packed(x3_c, y3_c), 2, 1, 1, 1),
            (split(by_y, by_x), 3, 1, 0, 1),
            (split(over_c(by_y), over_c(by_x)), 3, 1, 1, 1),
        ],
        sums,
        last=True,
    )
    mine, sums = after((mine, sums))
    moe_out, input_grad = (
        (mine[:, k : k + width] + back[:, k : k + width].astype(jnp.float32)).astype(back.dtype)
        for k in (0, width)
    )
    return (moe_out, input_grad, *sums)


def project_in(received, w_gate, w_up):
    gate = jnp.einsum("sjcd,jdf->sjcf", received, w_gate, preferred_element_type=jnp.float32)
    up = jnp.einsum("sjcd,jdf->sjcf", received, w_up, preferred_element_type=jnp.float32)
    return (gate, up)


def exchanged(tokens, expert_ids, route_weight, cotangent, w_gate, w_up, w_down):
    tok_rows, width = tokens.shape
    group = lax.axis_size("expert")
    local_exp = w_gate.shape[0]
    flat_ids = expert_ids.reshape(-1)
    onehot = (flat_ids[:, None] == jnp.arange(EXPERTS, dtype=jnp.int32)[None, :]).astype(jnp.int32)
    slot = jnp.sum((jnp.cumsum(onehot, axis=0) - onehot) * onehot, axis=1)
    target = flat_ids * CAP + slot
    token_pair = jnp.broadcast_to(tokens[:, None, :], (tok_rows, 2, width)).reshape(
        2 * tok_rows, width
    )
    outgoing = jnp.zeros((EXPERTS * CAP, width), jnp.bfloat16).at[target].set(token_pair)
    outgoing = outgoing.reshape(group, local_exp, CAP, width)
    received = lax.all_to_all(outgoing, "expert", split_axis=0, concat_axis=0, tiled=True)
    gate, up = project_in(received, w_gate, w_up)
    sig = jax.nn.sigmoid(gate)
    hidden = (gate * sig * up).astype(jnp.bfloat16)
    expert_out = jnp.einsum(
        "sjcf,jfd->sjcd", hidden, w_down, preferred_element_type=jnp.float32
    ).astype(jnp.bfloat16)
    returned = lax.all_to_all(
        expert_out, "expert", split_axis=0, concat_axis=0, tiled=True
    ).reshape(EXPERTS * CAP, width)
    picked = returned[target].reshape(tok_rows, 2, width).astype(jnp.float32)
    moe_out = jnp.sum(route_weight[:, :, None] * picked, axis=1).astype(jnp.bfloat16)
    cot_pair = jnp.broadcast_to(cotangent[:, None, :], (tok_rows, 2, width)).reshape(
        2 * tok_rows, width
    )
    scaled = (route_weight.reshape(-1)[:, None] * cot_pair.astype(jnp.float32)).astype(jnp.bfloat16)
    grad_out = jnp.zeros((EXPERTS * CAP, width), jnp.bfloat16).at[target].set(scaled)
    grad_out = grad_out.reshape(group, local_exp, CAP, width)
    drows = lax.all_to_all(grad_out, "expert", split_axis=0, concat_axis=0, tiled=True)
    dh = jnp.einsum("sjcd,jfd->sjcf", drows, w_down, preferred_element_type=jnp.float32)
    dgate = (dh * up * sig * (1.0 + gate * (1.0 - sig))).astype(jnp.bfloat16)
    dup = (dh * gate * sig).astype(jnp.bfloat16)
    dx_rows = jnp.einsum("sjcf,jdf->sjcd", dgate, w_gate, preferred_element_type=jnp.float32)
    dx_rows = (
        dx_rows + jnp.einsum("sjcf,jdf->sjcd", dup, w_up, preferred_element_type=jnp.float32)
    ).astype(jnp.bfloat16)
    dx_back = lax.all_to_all(dx_rows, "expert", split_axis=0, concat_axis=0, tiled=True).reshape(
        EXPERTS * CAP, width
    )
    input_grad = jnp.sum(
        dx_back[target].reshape(tok_rows, 2, width).astype(jnp.float32), axis=1
    ).astype(jnp.bfloat16)
    full_gate = jnp.einsum("sjcd,sjcf->jdf", received, dgate, preferred_element_type=jnp.float32)
    full_up = jnp.einsum("sjcd,sjcf->jdf", received, dup, preferred_element_type=jnp.float32)
    full_down = jnp.einsum("sjcf,sjcd->jfd", hidden, drows, preferred_element_type=jnp.float32)
    grads = [
        lax.psum_scatter(g, "dp", scatter_dimension=1, tiled=True)
        for g in (full_gate, full_up, full_down)
    ]
    return (moe_out, input_grad, *grads)


def solution(mesh):
    placed = (
        P(("dp", "expert"), None),
        P(("dp", "expert"), None),
        P(("dp", "expert"), None),
        P(("dp", "expert"), None),
        P("expert", None, None),
        P("expert", None, None),
        P("expert", None, None),
    )
    small = mesh.shape["dp"] == 8 and mesh.shape["expert"] == 4
    return jax.shard_map(
        gathered if small else exchanged,
        mesh=mesh,
        in_specs=placed,
        out_specs=(
            P(("dp", "expert"), None),
            P(("dp", "expert"), None),
            P("expert", "dp", None),
            P("expert", "dp", None),
            P("expert", "dp", None),
        ),
        check_vma=False,
    )
```

```python
import functools

import jax
import jax.numpy as jnp
from jax import lax
from jax.experimental import pallas as pl
from jax.experimental.pallas import tpu as pltpu
from jax.sharding import PartitionSpec as P

EXPERTS = 32
CAP = 24
VMEM_LIMIT = 22 * 1024 * 1024
SMALL_VMEM = 4 * 1024 * 1024
RING = 4


def route_kernel(ids_ref, rw_ref, out_ref):
    toks = ids_ref.shape[1]
    ids0, ids1 = ids_ref[0:1, :], ids_ref[1:2, :]
    expert = lax.broadcasted_iota(jnp.int32, (EXPERTS, toks), 0)
    hot0 = (expert == ids0).astype(jnp.float32)
    hot1 = (expert == ids1).astype(jnp.float32)
    row = lax.broadcasted_iota(jnp.int32, (toks, toks), 0)
    col = lax.broadcasted_iota(jnp.int32, (toks, toks), 1)
    earlier = (row < col).astype(jnp.bfloat16)
    before = jnp.dot(
        (hot0 + hot1).astype(jnp.bfloat16), earlier, preferred_element_type=jnp.float32
    )
    slot0 = jnp.sum(before * hot0, axis=0, keepdims=True)
    slot1 = jnp.sum(before * hot1, axis=0, keepdims=True)
    out_ref[0:1, :] = ids0.astype(jnp.float32) * CAP + slot0
    out_ref[1:2, :] = ids1.astype(jnp.float32) * CAP + slot1
    out_ref[2:4, :] = rw_ref[...]


def route(expert_ids, route_weight):
    toks = expert_ids.shape[0]
    return pl.pallas_call(
        route_kernel,
        out_shape=jax.ShapeDtypeStruct((4, toks), jnp.float32),
        compiler_params=pltpu.CompilerParams(vmem_limit_bytes=SMALL_VMEM),
    )(expert_ids.T, route_weight.T)


SMALL = pltpu.CompilerParams(vmem_limit_bytes=SMALL_VMEM)
FREE = pl.CostEstimate(flops=1, bytes_accessed=1, transcendentals=0)
VMEM = pl.BlockSpec(memory_space=pltpu.VMEM)
ANY = pl.BlockSpec(memory_space=pl.ANY)


def position():
    return lax.axis_index("dp"), lax.axis_index("expert")


def is_inner():
    z = position()[0] // 2
    return (z == 1) | (z == 2)


def join(a, b):
    def kernel(a_ref, b_ref, out_ref):
        out_ref[: a.shape[0]] = a_ref[...]
        out_ref[a.shape[0] :] = b_ref[...]

    return pl.pallas_call(
        kernel,
        in_specs=[VMEM] * 2,
        out_specs=VMEM,
        out_shape=jax.ShapeDtypeStruct((2 * a.shape[0],) + a.shape[1:], a.dtype),
        compiler_params=SMALL,
    )(a, b)


def pack(by, bx, block, at_ends=None):
    rows, width = block.shape[0], block.shape[1] // 2
    half = rows // 2
    choices = [block] if at_ends is None else [block, at_ends]

    def kernel(by_ref, bx_ref, *refs):
        block_refs, (px_ref, py_ref, sem) = refs[:-3], refs[-3:]
        copies = []
        for out_ref, ref, lane in ((px_ref, by_ref, width), (py_ref, bx_ref, 0)):
            for k in range(2):
                src = ref.at[pl.ds(k * half, half), pl.ds(lane, width)]
                copies.append((src, out_ref.at[pl.ds(rows, half), pl.ds(k * width, width)]))
        copies = [pltpu.make_async_copy(src, dst, sem.at[k]) for k, (src, dst) in enumerate(copies)]

        def tops(block_ref):
            return [
                pltpu.make_async_copy(block_ref, out_ref.at[pl.ds(0, rows)], sem.at[4 + k])
                for k, out_ref in enumerate((px_ref, py_ref))
            ]

        if len(block_refs) == 1:
            for c in tops(block_refs[0]):
                c.start()
        else:
            inner = is_inner()

            @pl.when(inner)
            def _():
                for c in tops(block_refs[0]):
                    c.start()

            @pl.when(jnp.logical_not(inner))
            def _():
                for c in tops(block_refs[1]):
                    c.start()

        for c in copies:
            c.start()
        for c in copies + tops(block_refs[0]):
            c.wait()

    return pl.pallas_call(
        kernel,
        in_specs=[ANY] * (2 + len(choices)),
        out_specs=[VMEM] * 2,
        out_shape=[pltpu.VMEM((rows + half, 2 * width), block.dtype)] * 2,
        scratch_shapes=[pltpu.SemaphoreType.DMA((6,))],
        compiler_params=SMALL,
    )(by, bx, *choices)


def beside(left, right):
    rows, width = left.shape

    def kernel(left_ref, right_ref, out_ref, sem):
        copies = [
            pltpu.make_async_copy(ref, out_ref.at[:, pl.ds(k * width, width)], sem.at[k])
            for k, ref in enumerate((left_ref, right_ref))
        ]
        for c in copies:
            c.start()
        for c in copies:
            c.wait()

    return pl.pallas_call(
        kernel,
        in_specs=[ANY] * 2,
        out_specs=VMEM,
        out_shape=pltpu.VMEM((rows, 2 * width), left.dtype),
        scratch_shapes=[pltpu.SemaphoreType.DMA((2,))],
        compiler_params=SMALL,
        cost_estimate=FREE,
    )(*in_hbm([left, right]))


def halves(a, b):
    rows, width = a.shape[0] * 2 // 3, a.shape[1] // 2

    def kernel(a_ref, b_ref, left_ref, right_ref, sem):
        top = pl.ds(0, rows)
        left = pltpu.make_async_copy(a_ref.at[top, pl.ds(0, width)], left_ref, sem.at[0])
        right = pltpu.make_async_copy(b_ref.at[top, pl.ds(width, width)], right_ref, sem.at[1])
        left.start()
        right.start()
        left.wait()
        right.wait()

    return pl.pallas_call(
        kernel,
        in_specs=[ANY] * 2,
        out_specs=[VMEM] * 2,
        out_shape=[pltpu.VMEM((rows, width), a.dtype)] * 2,
        scratch_shapes=[pltpu.SemaphoreType.DMA((2,))],
        compiler_params=SMALL,
    )(a, b)


def core_sum(keep, got):
    def kernel(keep_ref, got_ref, mine_ref, away_ref):
        mine_ref[...] = keep_ref[0].astype(jnp.float32) + got_ref[0].astype(jnp.float32)
        away_ref[...] = (keep_ref[1].astype(jnp.float32) + got_ref[1].astype(jnp.float32)).astype(
            away_ref.dtype
        )

    shape = keep.shape[1:]
    return pl.pallas_call(
        kernel,
        in_specs=[VMEM] * 2,
        out_specs=[VMEM] * 2,
        out_shape=[jax.ShapeDtypeStruct(shape, jnp.float32), jax.ShapeDtypeStruct(shape, keep.dtype)],
        compiler_params=pltpu.CompilerParams(vmem_limit_bytes=3 * SMALL_VMEM),
    )(keep, got)


def in_hbm(arrays):
    return [pltpu.with_memory_space_constraint(a, pltpu.HBM) for a in arrays]


def in_vmem(arrays):
    return [pltpu.with_memory_space_constraint(a, pltpu.VMEM) for a in arrays]


def load(*arrays):
    count, parts = len(arrays), arrays[0].shape[0]

    def kernel(*refs):
        sem = refs[-1]
        copies = [
            pltpu.make_async_copy(refs[k].at[j], refs[count + k].at[j], sem.at[k, j])
            for j in range(parts)
            for k in range(count)
        ]
        for c in copies:
            c.start()
        for c in copies:
            c.wait()

    return pl.pallas_call(
        kernel,
        in_specs=[ANY] * count,
        out_specs=[VMEM] * count,
        out_shape=[pltpu.VMEM(a.shape, a.dtype) for a in arrays],
        scratch_shapes=[pltpu.SemaphoreType.DMA((count, parts))],
        compiler_params=SMALL,
        cost_estimate=FREE,
    )(*in_hbm(arrays))


def pick_matrix(meta, base, slots):
    toks = meta.shape[1]
    place = lax.broadcasted_iota(jnp.int32, (slots, toks), 0)
    at0 = meta[0:1, :].astype(jnp.int32) - base
    at1 = meta[1:2, :].astype(jnp.int32) - base
    hit0, hit1 = place == at0, place == at1
    hot = jnp.where(hit0 | hit1, 1.0, 0.0).astype(jnp.bfloat16)
    weight = jnp.where(hit0, meta[2:3, :], 0.0) + jnp.where(hit1, meta[3:4, :], 0.0)
    return hot, jnp.sum(weight, axis=1, keepdims=True)


def dot(a, b, dims):
    return lax.dot_general(a, b, (dims, ((), ())), preferred_element_type=jnp.float32)


NN = ((1,), (0,))
NT = ((1,), (1,))
TN = ((0,), (0,))


def rows_kernel(pieces, n_arr, places, home, first, last, meta_ref, *refs):
    blocks = len(places)
    arrays, refs = refs[:n_arr], refs[n_arr:]
    wg_ref, wu_ref, wd_ref = refs[:3]
    refs = refs[3:]
    if not first:
        gg_in, gu_in, gd_in = refs[:3]
        refs = refs[3:]
    outs = refs[:3]
    refs = refs[3:]
    if home:
        keep_ref, send_ref = refs[:2]
        refs = refs[2:]
    tok_s, x_s, d_s, h_s, sem = refs[:5]
    refs = refs[5:]
    if last:
        sums, sem_out = refs[:3], refs[3]
        refs = refs[4:]
    else:
        sums = outs
    gg_ref, gu_ref, gd_ref = sums
    if home:
        hot_s, w_s, o_s = refs

    local_exp, width, ff = wg_ref.shape
    slots = local_exp * CAP
    replica, group = position()
    inner = is_inner()
    planes = (0, 4, jnp.where(inner, 20, 16), jnp.where(inner, 16, 20))
    sources = [planes[plane] + rest for plane, rest in places]
    base = group * slots

    ring = tok_s.shape[0]

    def fetch(b):
        for k, (sr, sc), (dr, dc), (nr, nc) in pieces[b]:
            src = arrays[k].at[pl.ds(sr, nr), pl.ds(sc, nc)]
            dst = tok_s.at[b % ring, pl.ds(dr, nr), pl.ds(dc, nc)]
            pltpu.make_async_copy(src, dst, sem.at[b % ring]).start()

    for b in range(min(ring, blocks)):
        fetch(b)

    for p in range(blocks // 2):
        pair = (2 * p, 2 * p + 1)
        hots, weights = [], []
        for b in pair:
            hot, weight = pick_matrix(meta_ref[sources[b]], base, slots)
            if home:
                hot_s[b] = hot
                w_s[b] = weight
            hots.append(hot)
            weights.append(weight)
        for b in pair:
            slot = tok_s.at[b % ring]
            pltpu.make_async_copy(slot, slot, sem.at[b % ring]).wait()
        chunk = 512
        for lane in range(0, 2 * width, chunk):
            got = [dot(hots[k], tok_s[pair[k] % ring, :, lane : lane + chunk], NN) for k in range(2)]
            if lane >= width:
                got = [got[k] * weights[k] for k in range(2)]
            for j in range(local_exp):
                rows = jnp.concatenate(
                    [got[k][j * CAP : (j + 1) * CAP] for k in range(2)], axis=0
                ).astype(jnp.bfloat16)
                to = slice(2 * p * CAP, 2 * (p + 1) * CAP)
                if lane < width:
                    x_s[j, to, lane : lane + chunk] = rows
                else:
                    d_s[j, to, lane - width : lane - width + chunk] = rows
        for b in pair:
            if b + ring < blocks:
                fetch(b + ring)

    def expert(j, carry):
        x, d = x_s[j], d_s[j]
        wg, wu, wd = wg_ref[j], wu_ref[j], wd_ref[j]
        gate = dot(x, wg, NN)
        up = dot(x, wu, NN)
        dh = dot(d, wd, NT)
        sig = jax.nn.sigmoid(gate)
        act = gate * sig
        hidden = (act * up).astype(jnp.bfloat16)
        dgate = (dh * up * sig * (1.0 + gate * (1.0 - sig))).astype(jnp.bfloat16)
        dup = (dh * act).astype(jnp.bfloat16)
        rows_g = gg_ref.shape[1]
        rows_d = gd_ref.shape[1]
        xs = x_s[j, :, pl.ds(pl.multiple_of(replica * rows_g, 128), rows_g)]
        both = dot(xs, jnp.concatenate([dgate, dup], axis=1), TN)
        gg, gu = both[:, :ff], both[:, ff:]
        h_s[...] = hidden
        per = 128 // rows_d
        hs = h_s[:, pl.ds(pl.multiple_of(replica // per * 128, 128), 128)]
        wide = dot(hs, d, TN)
        gd = wide[0:rows_d]
        for q in range(1, per):
            gd = jnp.where(replica % per == q, wide[q * rows_d : (q + 1) * rows_d], gd)
        if first:
            gg_ref[j], gu_ref[j], gd_ref[j] = gg, gu, gd
        else:
            gg_ref[j] = gg_in[j] + gg
            gu_ref[j] = gu_in[j] + gu
            gd_ref[j] = gd_in[j] + gd
        if last:
            for k in range(3):
                pltpu.make_async_copy(sums[k].at[j], outs[k].at[j], sem_out.at[k, j]).start()
        if home:
            out = dot(hidden, wd, NN)
            dx = dot(dgate, wg, NT) + dot(dup, wu, NT)
            to = pl.ds(pl.multiple_of(j * CAP, 8), CAP)
            for b in range(blocks):
                mine = slice(b * CAP, (b + 1) * CAP)
                o_s[b, to, :width] = out[mine] * w_s[b, to, :]
                o_s[b, to, width:] = dx[mine]
        return carry

    lax.fori_loop(0, local_exp, expert, 0)

    if home:
        half = blocks // 2
        for b in range(blocks):
            got = dot(hot_s[b], o_s[b].astype(jnp.bfloat16), TN).astype(jnp.bfloat16)
            if b < half:
                keep_ref[b] = got
            else:
                send_ref[b - half] = got
    if last:
        for j in range(local_exp):
            for k in range(3):
                pltpu.make_async_copy(sums[k].at[j], outs[k].at[j], sem_out.at[k, j]).wait()


def expert_rows(places, replicas, meta, parts, weights, sums, home=False, last=False):
    local_exp, width, ff = weights[0].shape
    blocks = len(parts)
    toks = meta.shape[2]
    first = sums is None
    slots = local_exp * CAP
    rows = blocks * CAP
    ring = 2 if home else min(blocks, RING)
    rows_g, rows_d = width // replicas, ff // replicas
    arrays, pieces = [], []
    for part in parts:
        mine = []
        for array, *where in part:
            found = [k for k, a in enumerate(arrays) if a is array]
            if not found:
                arrays.append(array)
            mine.append((found[0] if found else len(arrays) - 1, *where))
        pieces.append(tuple(mine))
    sum_shapes = [(local_exp, rows_g, ff), (local_exp, rows_g, ff), (local_exp, rows_d, width)]
    in_specs = [VMEM] + [ANY] * len(arrays) + [VMEM] * 3
    arrays = in_hbm(arrays)
    operands = [meta, *arrays, *in_vmem(weights)]
    aliases = {}
    if not first:
        if not last:
            aliases = {len(operands) + k: k for k in range(3)}
        in_specs += [VMEM] * 3
        operands += in_vmem(sums)
    if last:
        out_shape = [jax.ShapeDtypeStruct(s, jnp.float32) for s in sum_shapes]
        out_specs = [ANY] * 3
    else:
        out_shape = [pltpu.VMEM(s, jnp.float32) for s in sum_shapes]
        out_specs = [VMEM] * 3
    scratch = [
        pltpu.VMEM((ring, toks, 2 * width), jnp.bfloat16),
        pltpu.VMEM((local_exp, rows, width), jnp.bfloat16),
        pltpu.VMEM((local_exp, rows, width), jnp.bfloat16),
        pltpu.VMEM((rows, ff), jnp.bfloat16),
        pltpu.SemaphoreType.DMA((ring,)),
    ]
    if last:
        scratch += [pltpu.VMEM(s, jnp.float32) for s in sum_shapes]
        scratch += [pltpu.SemaphoreType.DMA((3, local_exp))]
    if home:
        out_shape += [jax.ShapeDtypeStruct((blocks // 2, toks, 2 * width), jnp.bfloat16)] * 2
        out_specs += [VMEM] * 2
        scratch += [
            pltpu.VMEM((blocks, slots, toks), jnp.bfloat16),
            pltpu.VMEM((blocks, slots, 1), jnp.float32),
            pltpu.VMEM((blocks, slots, 2 * width), jnp.float32),
        ]
    kernel = functools.partial(
        rows_kernel,
        tuple(pieces),
        len(arrays),
        tuple(places),
        home,
        first,
        last,
    )
    return pl.pallas_call(
        kernel,
        in_specs=in_specs,
        out_specs=out_specs,
        scratch_shapes=scratch,
        out_shape=out_shape,
        input_output_aliases=aliases,
        compiler_params=pltpu.CompilerParams(vmem_limit_bytes=VMEM_LIMIT),
        cost_estimate=FREE,
    )(*operands)


def gathered(tokens, expert_ids, route_weight, cotangent, w_gate, w_up, w_down):
    width = tokens.shape[1]
    local_exp = w_gate.shape[0]
    replicas, group = lax.axis_size("dp"), lax.axis_size("expert")
    axes = ("dp", "expert")
    def permute(value, move):
        pairs = []
        for dp in range(replicas):
            for ex in range(group):
                to = move(dp // 2, dp % 2, ex // 2, ex % 2)
                if to is not None:
                    tz, tx, ty, tc = to
                    pairs.append((dp * group + ex, (tz * 2 + tx) * group + ty * 2 + tc))
        return lax.ppermute(value, axes, pairs)

    over_x = lambda v: permute(v, lambda z, x, y, c: (z, 1 - x, y, c))
    over_y = lambda v: permute(v, lambda z, x, y, c: (z, x, 1 - y, c))
    over_c = lambda v: permute(v, lambda z, x, y, c: (z, x, y, 1 - c))
    near = lambda v: permute(v, lambda z, x, y, c: (z ^ 1, x, y, c))
    opposite = lambda v: permute(v, lambda z, x, y, c: (z ^ 2, x, y, c))
    mid = lambda v: permute(v, lambda z, x, y, c: (z ^ 3, x, y, c) if z in (1, 2) else None)
    outward = lambda v: permute(v, lambda z, x, y, c: (z ^ 1, x, y, c) if z in (1, 2) else None)

    own = beside(tokens, cotangent)
    toks = own.shape[0]
    half = toks // 2

    def whole(array):
        return ((array, (0, 0), (0, 0), (toks, 2 * width)),)

    def packed(px, py):
        return tuple(
            (array, (toks, k * width), (k * half, lane), (half, width))
            for array, lane in ((py, 0), (px, width))
            for k in range(2)
        )

    def split(left, right):
        return (left, (0, 0), (0, 0), (toks, width)), (right, (0, 0), (0, width), (toks, width))

    def rows(meta, blocks, sums, **kind):
        parts = [b[0] for b in blocks]
        places = [(z, c + y * 2 + x * 8) for _, z, x, c, y in blocks]
        return expert_rows(places, replicas, meta, parts, weights, sums, **kind)

    after = lax.optimization_barrier

    meta = route(expert_ids, route_weight)[None]
    meta_c = over_c(meta)
    bx0, by0, d1, m1 = over_x(own), over_y(own), near(own), mid(own)
    meta = join(meta, meta_c)
    meta_y = over_y(meta)
    weights = load(w_gate, w_up, w_down)

    by0, bx0, d1, meta_y, weights, own_late = after((by0, bx0, d1, meta_y, weights, own))
    px1, py1 = pack(by0, bx0, d1)
    x1, y1, e1, m2 = over_x(px1), over_y(py1), outward(m1), mid(d1)
    meta_home = join(meta, meta_y)
    meta_here = join(meta_home, near(meta_home))
    meta_x = over_x(meta_here)
    own_c, by0_c = over_c(own_late), over_c(by0)
    *sums, keep, send = rows(
        meta_home,
        [
            (split(tokens, cotangent), 0, 0, 0, 0),
            (whole(by0), 0, 0, 0, 1),
            (whole(own_c), 0, 0, 1, 0),
            (whole(by0_c), 0, 0, 1, 1),
        ],
        None,
        home=True,
    )

    keep, send, x1, y1, e1, m2, meta_x, sums = after((keep, send, x1, y1, e1, m2, meta_x, sums))
    px2, py2 = pack(y1, x1, m1, at_ends=e1)
    px2, py2, x1, y1, bx0, d1 = after((px2, py2, x1, y1, bx0, d1))
    x2, y2, e2 = over_x(px2), over_y(py2), outward(m2)
    meta_half = join(meta_here, meta_x)
    meta_far = opposite(meta_half)
    x1_c, y1_c, bx0_c, d1_c = over_c(x1), over_c(y1), over_c(bx0), over_c(d1)
    sums = rows(
        meta_half,
        [
            (whole(bx0), 0, 1, 0, 0),
            (whole(bx0_c), 0, 1, 1, 0),
            (whole(x1), 1, 1, 0, 0),
            (whole(x1_c), 1, 1, 1, 0),
            (whole(y1), 1, 0, 0, 1),
            (whole(y1_c), 1, 0, 1, 1),
            (packed(x1, y1), 0, 1, 0, 1),
            (packed(x1_c, y1_c), 0, 1, 1, 1),
        ],
        sums,
    )

    x2, y2, e2, meta_far, d1_c, sums = after((x2, y2, e2, meta_far, d1_c, sums))
    px3, py3 = pack(y2, x2, m2, at_ends=e2)
    px3, py3, x2, y2, px2, send = after((px3, py3, x2, y2, px2, send))
    x3, y3 = over_x(px3), over_y(py3)
    meta_all = join(meta_half, meta_far)
    x2_c, y2_c, got = over_c(x2), over_c(y2), over_c(send)
    px2_c, px3_c = over_c(px2), over_c(px3)
    mine, away = core_sum(keep, got)
    sums = rows(
        meta_all,
        [
            (whole(d1), 1, 0, 0, 0),
            (whole(d1_c), 1, 0, 1, 0),
            (whole(x2), 2, 1, 0, 0),
            (whole(x2_c), 2, 1, 1, 0),
            (whole(y2), 2, 0, 0, 1),
            (whole(y2_c), 2, 0, 1, 1),
            (packed(x2, y2), 1, 1, 0, 1),
            (packed(x2_c, y2_c), 1, 1, 1, 1),
        ],
        sums,
    )

    x3, y3, px2_c, px3_c, away, sums = after((x3, y3, px2_c, px3_c, away, sums))
    left, right = halves(x3, y3)
    by_y, by_x = over_y(left), over_x(right)
    back = over_y(away)
    x3_c, y3_c = over_c(x3), over_c(y3)
    sums = rows(
        meta_all,
        [
            (whole(px2), 2, 0, 0, 0),
            (whole(px2_c), 2, 0, 1, 0),
            (whole(px3), 3, 0, 0, 0),
            (whole(px3_c), 3, 0, 1, 0),
            (whole(x3), 3, 1, 0, 0),
            (whole(y3), 3, 0, 0, 1),
        ],
        sums,
    )

    by_y, by_x, sums = after((by_y, by_x, sums))
    sums = rows(
        meta_all,
        [
            (whole(x3_c), 3, 1, 1, 0),
            (whole(y3_c), 3, 0, 1, 1),
            (packed(x3, y3), 2, 1, 0, 1),
            (packed(x3_c, y3_c), 2, 1, 1, 1),
            (split(by_y, by_x), 3, 1, 0, 1),
            (split(over_c(by_y), over_c(by_x)), 3, 1, 1, 1),
        ],
        sums,
        last=True,
    )
    mine, sums = after((mine, sums))
    moe_out, input_grad = (
        (mine[:, k : k + width] + back[:, k : k + width].astype(jnp.float32)).astype(back.dtype)
        for k in (0, width)
    )
    return (moe_out, input_grad, *sums)


def project_in(received, w_gate, w_up):
    gate = jnp.einsum("sjcd,jdf->sjcf", received, w_gate, preferred_element_type=jnp.float32)
    up = jnp.einsum("sjcd,jdf->sjcf", received, w_up, preferred_element_type=jnp.float32)
    return (gate, up)


def exchanged(tokens, expert_ids, route_weight, cotangent, w_gate, w_up, w_down):
    tok_rows, width = tokens.shape
    group = lax.axis_size("expert")
    local_exp = w_gate.shape[0]
    flat_ids = expert_ids.reshape(-1)
    onehot = (flat_ids[:, None] == jnp.arange(EXPERTS, dtype=jnp.int32)[None, :]).astype(jnp.int32)
    slot = jnp.sum((jnp.cumsum(onehot, axis=0) - onehot) * onehot, axis=1)
    target = flat_ids * CAP + slot
    token_pair = jnp.broadcast_to(tokens[:, None, :], (tok_rows, 2, width)).reshape(
        2 * tok_rows, width
    )
    outgoing = jnp.zeros((EXPERTS * CAP, width), jnp.bfloat16).at[target].set(token_pair)
    outgoing = outgoing.reshape(group, local_exp, CAP, width)
    received = lax.all_to_all(outgoing, "expert", split_axis=0, concat_axis=0, tiled=True)
    gate, up = project_in(received, w_gate, w_up)
    sig = jax.nn.sigmoid(gate)
    hidden = (gate * sig * up).astype(jnp.bfloat16)
    expert_out = jnp.einsum(
        "sjcf,jfd->sjcd", hidden, w_down, preferred_element_type=jnp.float32
    ).astype(jnp.bfloat16)
    returned = lax.all_to_all(
        expert_out, "expert", split_axis=0, concat_axis=0, tiled=True
    ).reshape(EXPERTS * CAP, width)
    picked = returned[target].reshape(tok_rows, 2, width).astype(jnp.float32)
    moe_out = jnp.sum(route_weight[:, :, None] * picked, axis=1).astype(jnp.bfloat16)
    cot_pair = jnp.broadcast_to(cotangent[:, None, :], (tok_rows, 2, width)).reshape(
        2 * tok_rows, width
    )
    scaled = (route_weight.reshape(-1)[:, None] * cot_pair.astype(jnp.float32)).astype(jnp.bfloat16)
    grad_out = jnp.zeros((EXPERTS * CAP, width), jnp.bfloat16).at[target].set(scaled)
    grad_out = grad_out.reshape(group, local_exp, CAP, width)
    drows = lax.all_to_all(grad_out, "expert", split_axis=0, concat_axis=0, tiled=True)
    dh = jnp.einsum("sjcd,jfd->sjcf", drows, w_down, preferred_element_type=jnp.float32)
    dgate = (dh * up * sig * (1.0 + gate * (1.0 - sig))).astype(jnp.bfloat16)
    dup = (dh * gate * sig).astype(jnp.bfloat16)
    dx_rows = jnp.einsum("sjcf,jdf->sjcd", dgate, w_gate, preferred_element_type=jnp.float32)
    dx_rows = (
        dx_rows + jnp.einsum("sjcf,jdf->sjcd", dup, w_up, preferred_element_type=jnp.float32)
    ).astype(jnp.bfloat16)
    dx_back = lax.all_to_all(dx_rows, "expert", split_axis=0, concat_axis=0, tiled=True).reshape(
        EXPERTS * CAP, width
    )
    input_grad = jnp.sum(
        dx_back[target].reshape(tok_rows, 2, width).astype(jnp.float32), axis=1
    ).astype(jnp.bfloat16)
    full_gate = jnp.einsum("sjcd,sjcf->jdf", received, dgate, preferred_element_type=jnp.float32)
    full_up = jnp.einsum("sjcd,sjcf->jdf", received, dup, preferred_element_type=jnp.float32)
    full_down = jnp.einsum("sjcf,sjcd->jfd", hidden, drows, preferred_element_type=jnp.float32)
    grads = [
        lax.psum_scatter(g, "dp", scatter_dimension=1, tiled=True)
        for g in (full_gate, full_up, full_down)
    ]
    return (moe_out, input_grad, *grads)


def solution(mesh):
    placed = (
        P(("dp", "expert"), None),
        P(("dp", "expert"), None),
        P(("dp", "expert"), None),
        P(("dp", "expert"), None),
        P("expert", None, None),
        P("expert", None, None),
        P("expert", None, None),
    )
    small = mesh.shape["dp"] == 8 and mesh.shape["expert"] == 4
    return jax.shard_map(
        gathered if small else exchanged,
        mesh=mesh,
        in_specs=placed,
        out_specs=(
            P(("dp", "expert"), None),
            P(("dp", "expert"), None),
            P("expert", "dp", None),
            P("expert", "dp", None),
            P("expert", "dp", None),
        ),
        check_vma=False,
    )
```
